256 devices in a mesh: space: 32 (over z, x), state: 8 (over y, core).
Axes of the slice: x: 4, y: 4, z: 8, core: 2. Of those that a mesh axis runs over, the one named last changes fastest.
Arguments:
- states: float32 [64, 524288], P('state', 'space')
- bounds: float32 [3], replicated, as said below
- element_matrix: float32 [250, 125], replicated
- elem_nodes: int32 [125, 8192], P(None, 'space'), may hold values from 0 to 20479, as said below
- face_nodes: int32 [131072], P('space'), may hold values from 0 to 16383, as said below
- kinetic: float32 [8192], P('space'), may hold values from 0.5 to 4
- potential: float32 [8192], P('space'), may hold values from -1 to 0.5
- elem_count: int32 [32], P('space'), may hold values from 64 to 256, as said below
Outputs:
- filtered: float32 [64, 524288], P('state', 'space')
- margin: float32 [64, 64], P('state')
The draws below stay inside these ranges and needn't reach their ends.
Inputs may be any that keep to these rules, and one draw needn't show every extreme that they name: `elem_nodes`: within each partition's 256 columns, rows 0 to 99 of a column are local node indices below 16384, and rows 100 to 124 are 16384 plus a face position below 4096. The entries of one column are distinct. `face_nodes`: within each partition's 4096 entries, distinct local node indices. `elem_count`: some partition has all 256 slots live in every draw. `bounds`: a0 < lo < hi.
All inputs are finite; a program needn't handle non-finite values.
Results may differ from the reference program's by a relative error of at most 0.0018.
Values may be sent and summed in bfloat16 or wider, within the bound.
A program may use at most 128 MiB of HBM per device.

```python
import math
import jax
import jax.numpy as jnp
from jax import lax

STATES = 64
NPE = 125
DEG = 4
LAT = 64
FACE = 4096
NLOC = 16384
ESLOT = 256
NODES = 524288
N_SPACE = 32


def node_layout(key):
    node_keys = jax.random.split(jax.random.fold_in(key, 7), N_SPACE)
    node_perms = jax.vmap(lambda k: jax.random.permutation(k, NLOC))(node_keys)
    slot_keys = jax.random.split(jax.random.fold_in(key, 8), N_SPACE)
    slot_perms = jax.vmap(lambda k: jax.random.permutation(k, ESLOT))(slot_keys)
    return (node_perms.astype(jnp.int32), slot_perms.astype(jnp.int32))


def draw_elem_nodes(key, part):
    node_perms, slot_perms = node_layout(key)
    side = LAT // 4
    corner = jnp.arange(125, dtype=jnp.int32)
    layer = corner // 25
    across = corner // 5 % 5
    along = corner % 5
    elem_row = slot_perms // side
    elem_col = slot_perms % side
    row_pos = (4 * elem_row[:, None, :] + across[None, :, None]) % LAT
    col_pos = (4 * elem_col[:, None, :] + along[None, :, None]) % LAT
    flat_pos = row_pos * LAT + col_pos
    owned_pos = jnp.minimum(layer, 3)[None, :, None] * (LAT * LAT) + flat_pos
    owned = jax.vmap(lambda perm, idx: perm[idx])(node_perms, owned_pos)
    result = jnp.where(layer[None, :, None] == 4, NLOC + flat_pos, owned)
    return result.transpose(1, 0, 2).reshape(125, N_SPACE * ESLOT).astype(jnp.int32)


def draw_face_nodes(key, part):
    node_perms, slot_perms = node_layout(key)
    return node_perms[:, :FACE].reshape(N_SPACE * FACE).astype(jnp.int32)


def draw_elem_count(key, part):
    first_key, second_key = jax.random.split(jax.random.fold_in(key, 3))
    counts = jax.random.randint(first_key, (N_SPACE,), ESLOT // 4, ESLOT + 1)
    fullest = jax.random.randint(second_key, (), 0, N_SPACE)
    counts = counts.at[fullest].set(ESLOT)
    counts = counts.at[(fullest + 1) % N_SPACE].set(ESLOT // 4)
    return counts.astype(jnp.int32)


def draw_states(key, part):
    key_a, key_b, key_c = jax.random.split(jax.random.fold_in(key, 5), 3)
    node = jnp.arange(N_SPACE * NLOC, dtype=jnp.int32)
    owner = (node // NLOC).astype(jnp.float32)
    noise = jax.random.normal(key_a, (STATES, N_SPACE * NLOC), jnp.float32)
    shared = jax.random.normal(key_b, (N_SPACE * NLOC,), jnp.float32)
    weights = jax.random.normal(key_c, (STATES, 1), jnp.float32)
    rise = 1.0 + 2.0 * owner / (N_SPACE - 1)
    return (1.2 * rise[None, :] * (weights * shared[None, :] + noise)).astype(jnp.float32)


def draw_element_matrix(key, part):
    noise_key = jax.random.fold_in(key, 9)
    noise = jax.random.normal(noise_key, (2, 125, 125), jnp.float32)
    symmetric = (noise + jnp.swapaxes(noise, 1, 2)) * 0.7071
    index = jnp.arange(125, dtype=jnp.int32)
    identity = (index[:, None] == index[None, :]).astype(jnp.float32)
    stiffness = 0.05 * symmetric[0] + 1.3 * identity
    mass = 0.02 * symmetric[1] + 0.5 * identity
    return jnp.concatenate([stiffness, mass], axis=0).astype(jnp.float32)


def draw_bounds(key, part):
    key_a, key_b, key_c = jax.random.split(jax.random.fold_in(key, 4), 3)
    lowest = jax.random.uniform(key_a, (), jnp.float32, -1.0, 0.0)
    lower = lowest + jax.random.uniform(key_b, (), jnp.float32, 1.5, 3.0)
    upper = jax.random.uniform(key_c, (), jnp.float32, 12.0, 20.0)
    return jnp.stack([lowest, lower, upper]).astype(jnp.float32)


def levels(own_key, dims, pieces, least, largest):
    factor_of = 1.0
    for axis_at, blocks in pieces:
        steps = jax.random.uniform(jax.random.fold_in(jax.random.fold_in(own_key, 6), axis_at), (blocks,), jnp.float32, least / len(pieces), largest / len(pieces))
        factor_of = factor_of * jnp.repeat(jnp.exp(steps), dims[axis_at] // blocks).reshape((-1,) + (1,) * (len(dims) - 1 - axis_at))
    return factor_of


def setup_inputs(seed: int = 0) -> dict:
    key_list = jax.random.split(jax.random.key(seed), 9)
    states = draw_states(jax.random.fold_in(key_list[8], 71), 0)
    bounds = draw_bounds(jax.random.fold_in(key_list[8], 71), 0)
    element_matrix = draw_element_matrix(jax.random.fold_in(key_list[8], 71), 0)
    elem_nodes = draw_elem_nodes(jax.random.fold_in(key_list[8], 71), 0)
    face_nodes = draw_face_nodes(jax.random.fold_in(key_list[8], 71), 0)
    kinetic = jnp.clip(jnp.exp(math.log(4.0) - 2.0794415 * jax.random.uniform(key_list[5], (N_SPACE * ESLOT,), jnp.float32) ** levels(key_list[5], (N_SPACE * ESLOT,), ((0, 32),), -0.2, 0.2)), 0.5, 4.0)
    potential = jnp.clip(-1.0 + 1.5 * jax.random.uniform(key_list[6], (N_SPACE * ESLOT,), jnp.float32) ** levels(key_list[6], (N_SPACE * ESLOT,), ((0, 32),), -0.2, 0.2), -1.0, 0.5)
    elem_count = draw_elem_count(jax.random.fold_in(key_list[8], 71), 0)
    return {"states": states, "bounds": bounds, "element_matrix": element_matrix, "elem_nodes": elem_nodes, "face_nodes": face_nodes, "kinetic": kinetic, "potential": potential, "elem_count": elem_count}


def apply_hamiltonian(block, elem_nodes, face_nodes, kin_live, pot_live, element_matrix):
    width = block.shape[0]
    spread = block.reshape(width, N_SPACE, NLOC)
    faces = face_nodes.reshape(N_SPACE, FACE)
    face_vals = jnp.take_along_axis(spread, faces[None].astype(jnp.int32), axis=2)
    ghosts = jnp.concatenate([face_vals[:, 1:], jnp.zeros((width, 1, FACE), jnp.float32)], axis=1)
    extended = jnp.concatenate([spread, ghosts], axis=2).transpose(1, 0, 2)
    slots = elem_nodes.reshape(NPE, N_SPACE, ESLOT).transpose(1, 0, 2)

    def one_partition(args):
        ext_part, slot_nodes, kin_part, pot_part = args
        gathered = ext_part[:, slot_nodes]
        product = jnp.einsum("kb,sbe->ske", element_matrix, gathered, precision=lax.Precision.HIGHEST)
        contrib = kin_part * product[:, :NPE] + pot_part * product[:, NPE:]
        return jnp.zeros((width, NLOC + FACE), jnp.float32).at[:, slot_nodes].add(contrib)

    summed = lax.map(one_partition, (extended, slots, kin_live, pot_live))
    local_part = summed[:, :, :NLOC]
    ghost_part = summed[:, :, NLOC:]
    incoming = jnp.concatenate([jnp.zeros((1, width, FACE), jnp.float32), ghost_part[:-1]], axis=0)
    local_part = jax.vmap(lambda own_vals, face_idx, extra: own_vals.at[:, face_idx].add(extra))(local_part, faces, incoming)
    return local_part.transpose(1, 0, 2).reshape(width, N_SPACE * NLOC)


def reference(states, bounds, element_matrix, elem_nodes, face_nodes, kinetic, potential, elem_count):
    slot_ids = jnp.arange(ESLOT, dtype=jnp.int32)
    alive = (slot_ids[None, :] < elem_count[:, None]).astype(jnp.float32)
    kin_live = 0.5 * kinetic.reshape(N_SPACE, ESLOT) * alive
    pot_live = potential.reshape(N_SPACE, ESLOT) * alive

    def hamiltonian(block):
        return apply_hamiltonian(block, elem_nodes, face_nodes, kin_live, pot_live, element_matrix)

    lowest, lower, upper = bounds[0], bounds[1], bounds[2]
    half_width = (upper - lower) / 2.0
    center = (upper + lower) / 2.0
    sigma_now = half_width / (lowest - center)
    gamma_ratio = 2.0 / sigma_now
    previous = states
    current = (hamiltonian(states) - center * states) * (sigma_now / half_width)
    for repeat in range(DEG - 1):
        sigma_next = 1.0 / (gamma_ratio - sigma_now)
        following = (hamiltonian(current) - center * current) * (2.0 * sigma_next / half_width) - (sigma_now * sigma_next) * previous
        previous = current
        current = following
        sigma_now = sigma_next
    rounded = current.astype(jnp.bfloat16)
    margin = jnp.dot(rounded, rounded.T, preferred_element_type=jnp.float32) / NODES
    return current, margin
```

```python
import functools

import jax
import jax.numpy as jnp
import numpy as np
from jax import lax
from jax.experimental import pallas as pl
from jax.experimental.pallas import tpu as pltpu
from jax.sharding import PartitionSpec as P

DEG = 4
G = 8
W = 16
LANES = G * W
KU = 5
MESH = pl.DeviceIdType.MESH
F32 = jnp.float32
BF16 = jnp.bfloat16
VMEM_LIMIT = 58 * 2**20


def expand_matrix():
    l = np.arange(LANES)[:, None]
    m = np.arange(G * LANES)[None, :]
    one = (l // W == m // LANES) & (l % W == m % W)
    return jnp.asarray(np.concatenate([one, one], 0), BF16)


def fold_matrix():
    j = np.arange(G)[:, None, None, None]
    l = np.arange(LANES)[None, None, :, None]
    m = np.arange(LANES)[None, None, None, :]
    one = (m // W == j) & (m % W == l % W)
    one = np.broadcast_to(one, (G, 2, LANES, LANES))
    return jnp.asarray(one.reshape(G * 2 * LANES, LANES), BF16)


def split(value):
    high = value.astype(BF16)
    low = (value - high.astype(F32)).astype(BF16)
    return high, low


def lane_group():
    return lax.broadcasted_iota(jnp.int32, (1, LANES), 1) // W


def merge_groups(rows):
    step = 1
    group = lane_group()
    while len(rows) > 1:
        odd = (group // step) % 2 == 1
        rows = [jnp.where(odd, rows[a + 1], rows[a]) for a in range(0, len(rows), 2)]
        step *= 2
    return rows[0]


def expand_section(src, src_at, dst, dst_at, count, emat):
    block = 256

    def step(i, carry):
        q = pl.multiple_of(i * block, block)
        high, low = split(src[pl.ds(src_at + q, block), :])
        wide = jnp.dot(
            jnp.concatenate([high, low], axis=1), emat[...], preferred_element_type=F32
        )
        for j in range(G):
            dst[pl.ds(dst_at + j * count + q, block), :] = wide[:, j * LANES : (j + 1) * LANES]
        return carry

    lax.fori_loop(0, count // block, step, 0)


def start_lists(source, lists, sems):
    copies = [
        pltpu.make_async_copy(source.at[k], lists[k], sems.at[k]) for k in range(len(lists))
    ]
    for copy in copies:
        copy.start()
    return copies


def setup_kernel(
    nmain, nface, first, second, face_row, face_hbm, raw, emat, out, face_send, slots, X, sems, *faces
):
    qmain, qface = nmain // G, nface // G
    copies = start_lists(face_hbm, faces, sems)
    hi_count = nmain // 128
    chunk = 1024
    table = jnp.zeros((256, hi_count), F32)
    for at in range(0, nface, chunk):
        node = face_row[:, at : at + chunk]
        pos = lax.broadcasted_iota(jnp.int32, (1, chunk), 1) + (at + 1)
        low = lax.broadcasted_iota(jnp.int32, (128, chunk), 0) == (node & 127)
        high = lax.broadcasted_iota(jnp.int32, (hi_count, chunk), 0) == (node >> 7)
        big = jnp.where(low, (pos >> 6).astype(F32), 0.0)
        small = jnp.where(low, (pos & 63).astype(F32), 0.0)
        table += lax.dot_general(
            jnp.concatenate([big, small], axis=0).astype(BF16),
            high.astype(F32).astype(BF16),
            (((1,), (1,)), ((), ())),
            preferred_element_type=F32,
        )
    table = table.astype(BF16)
    width = raw.shape[1]
    owned = (KU - 1) * G
    for k in range(owned):
        node = raw[k : k + 1, :]
        high = lax.broadcasted_iota(jnp.int32, (hi_count, width), 0) == (node >> 7)
        got = jnp.dot(table, high.astype(F32).astype(BF16), preferred_element_type=F32)
        both = got[:128] * 64.0 + got[128:]
        low = lax.broadcasted_iota(jnp.int32, (128, width), 0) == (node & 127)
        pos = jnp.sum(jnp.where(low, both, 0.0), axis=0, keepdims=True).astype(jnp.int32)
        slots[k : k + 1, :] = jnp.where(pos > 0, nmain + pos - 1, node)
    slots[owned:, :] = raw[owned:, :] + nface
    def turn(i, carry):
        q = pl.multiple_of(i * 128, 128)
        parts = []
        for j in range(G):
            parts.append(first[:, pl.ds(j * qmain + q, 128)])
            parts.append(second[:, pl.ds(j * qmain + q, 128)])
        out[pl.ds(q, 128), :] = jnp.concatenate(parts, axis=0).T
        return carry

    lax.fori_loop(0, qmain // 128, turn, 0)
    expand_section(out, 0, X, 0, qmain, emat)
    for copy in copies:
        copy.wait()
    zero = jnp.zeros((1, LANES), F32)

    def take(q, carry):
        nodes = [faces[j][q] for j in range(G)]
        out[pl.ds(qmain + q, 1), :] = merge_groups([X[pl.ds(n, 1), :] for n in nodes])
        for n in nodes:
            X[pl.ds(n, 1), :] = zero
        return carry

    lax.fori_loop(0, qface, take, 0, unroll=4)

    def pack(i, carry):
        q = pl.multiple_of(i * 8, 8)
        out[pl.ds(q, 8), :] = merge_groups([X[pl.ds(j * qmain + q, 8), :] for j in range(G)])
        return carry

    lax.fori_loop(0, qmain // 8, pack, 0, unroll=4)
    face_send[...] = out[qmain : qmain + qface, :].astype(BF16)


def setup(first, second, face_nodes, raw, emat):
    nmain, nface = first.shape[1], face_nodes.shape[0]
    qmain, qface = nmain // G, nface // G
    vmem = pl.BlockSpec(memory_space=pltpu.VMEM)
    return pl.pallas_call(
        functools.partial(setup_kernel, nmain, nface),
        name="setup_rows",
        out_shape=[
            jax.ShapeDtypeStruct((qmain + qface, LANES), F32),
            jax.ShapeDtypeStruct((qface, LANES), BF16),
            jax.ShapeDtypeStruct(raw.shape, jnp.int32),
        ],
        in_specs=[vmem, vmem, vmem, pl.BlockSpec(memory_space=pl.ANY), vmem, vmem],
        out_specs=[vmem, vmem, vmem],
        scratch_shapes=[
            pltpu.VMEM((nmain, LANES), F32),
            pltpu.SemaphoreType.DMA((G,)),
        ]
        + [pltpu.SMEM((qface,), jnp.int32)] * G,
        compiler_params=pltpu.CompilerParams(vmem_limit_bytes=VMEM_LIMIT),
    )(first, second, face_nodes.reshape(1, nface), face_nodes.reshape(G, qface), raw, emat)


def element_kernel(
    sections, chunks, steps, mainface, ghost, slots_hbm, mcat, kin, pot, emat, fmat,
    part, X, acc0, acc1, U, Y, sems, *lists,
):
    copies = start_lists(slots_hbm, lists, sems)
    accs = (acc0, acc1)
    at = 0
    src, src_at = mainface, 0
    for i, count in enumerate(sections):
        if i == 2:
            src, src_at = ghost, 0
        expand_section(src, src_at, X, at, count, emat)
        at += G * count
        src_at += count
    total = at
    zero = jnp.zeros((64, LANES), F32)

    def clear(i, carry):
        q = pl.multiple_of(i * 64, 64)
        acc0[pl.ds(q, 64), :] = zero
        acc1[pl.ds(q, 64), :] = zero
        return carry

    lax.fori_loop(0, total // 64, clear, 0)
    U[...] = jnp.zeros_like(U)
    for copy in copies:
        copy.wait()
    group = lane_group()
    masks = [group == j for j in range(G)]

    def gather(c, r):
        t = c * steps + r
        for b in range(KU):
            rows = [X[pl.ds(lists[b * G + j][t], 1), :] for j in range(G)]
            U[pl.ds(b * steps + r, 1), :] = merge_groups(rows)

    def scatter(c, r):
        t = c * steps + r
        for b in range(KU):
            acc = accs[b % 2]
            y = Y[pl.ds(b * steps + r, 1), :]
            nodes = [lists[b * G + j][t] for j in range(G)]
            sums = [acc[pl.ds(n, 1), :] + y for n in nodes]
            for j in range(G):
                pltpu.store(acc.at[pl.ds(nodes[j], 1), :], sums[j], mask=masks[j])

    def product(c):
        high, low = split(U[...])
        prod = jnp.dot(
            mcat[...], jnp.concatenate([high, high, low], axis=0), preferred_element_type=F32
        )
        Y[...] = kin[pl.ds(c, 1), :] * prod[:128] + pot[pl.ds(c, 1), :] * prod[128:]

    def first(r, carry):
        gather(0, r)
        return carry

    lax.fori_loop(0, steps, first, 0)

    def chunk(c, carry):
        product(c)

        def step(r, inner):
            gather(c + 1, r)
            scatter(c, r)
            return inner

        lax.fori_loop(0, steps, step, 0)
        return carry

    lax.fori_loop(0, chunks - 1, chunk, 0)
    product(chunks - 1)

    def last(r, carry):
        scatter(chunks - 1, r)
        return carry

    lax.fori_loop(0, steps, last, 0)
    at, out_at = 0, 0
    block = 256
    for count in sections:

        def fold(i, carry, at=at, out_at=out_at, count=count):
            q = pl.multiple_of(i * block, block)
            pieces = []
            for j in range(G):
                rows = pl.ds(at + j * count + q, block)
                pieces.extend(split(acc0[rows, :] + acc1[rows, :]))
            part[pl.ds(out_at + q, block), :] = jnp.dot(
                jnp.concatenate(pieces, axis=1), fmat[...], preferred_element_type=F32
            )
            return carry

        lax.fori_loop(0, count // block, fold, 0)
        at += G * count
        out_at += count


def elements(mainface, ghost, slots, mcat, kin, pot, emat, fmat, qmain, steps):
    qface = mainface.shape[0] - qmain
    sections = (qmain, qface, ghost.shape[0])
    total = sum(sections)
    chunks = kin.shape[0]
    vmem = pl.BlockSpec(memory_space=pltpu.VMEM)
    return pl.pallas_call(
        functools.partial(element_kernel, sections, chunks, steps),
        name="element_rows",
        out_shape=jax.ShapeDtypeStruct((total, LANES), F32),
        in_specs=[vmem, vmem, pl.BlockSpec(memory_space=pl.ANY)] + [vmem] * 5,
        out_specs=vmem,
        scratch_shapes=[
            pltpu.VMEM((G * total, LANES), F32),
            pltpu.VMEM((G * total, LANES), F32),
            pltpu.VMEM((G * total, LANES), F32),
            pltpu.VMEM((128, LANES), F32),
            pltpu.VMEM((128, LANES), F32),
            pltpu.SemaphoreType.DMA((KU * G,)),
        ]
        + [pltpu.SMEM((slots.shape[1],), jnp.int32)] * (KU * G),
        compiler_params=pltpu.CompilerParams(vmem_limit_bytes=VMEM_LIMIT),
    )(mainface, ghost, slots, mcat, kin, pot, emat, fmat)


def exchange_kernel(
    qmain, qface, parts, coef, part, cur, cur_ghost, prev, prev_ghost, out, out_ghost,
    own, theirs, new, new_ghost, up_send, down_send, from_below, from_above,
    load_sem, store_sem, send_sem, recv_sem, side_send, side_recv, relay_send, relay_recv,
):
    pieces = 4
    rows = qmain // pieces
    half = qface // 2
    space, state = lax.axis_index("space"), lax.axis_index("state")
    core = lax.rem(state, 2)
    other = state + 1 - 2 * core
    above = lax.rem(space + 1, parts)
    below = lax.rem(space + parts - 1, parts)
    load = pltpu.make_async_copy(part, own, load_sem)
    load.start()
    barrier = pltpu.get_barrier_semaphore()
    for device in ((space, other), (above, state), (below, state)):
        pl.semaphore_signal(barrier, inc=1, device_id=device, device_id_type=MESH)
    pl.semaphore_wait(barrier, 3)

    mine = pl.multiple_of(core * half, half)
    not_mine = pl.multiple_of((1 - core) * half, half)
    face_at, ghost_at = qmain, qmain + qface
    spans = (
        [pl.ds(face_at + not_mine, half), pl.ds(ghost_at + not_mine, half)]
        + [pl.ds(i * rows, rows) for i in range(pieces)]
        + [pl.ds(face_at + mine, half), pl.ds(ghost_at + mine, half)]
    )
    swaps = []
    for i, span in enumerate(spans):
        swap = pltpu.make_async_remote_copy(
            src_ref=part.at[span, :], dst_ref=theirs.at[span, :],
            send_sem=send_sem.at[i], recv_sem=recv_sem.at[i],
            device_id=(space, other), device_id_type=MESH,
        )
        swap.start()
        swaps.append(swap)

    def arrived(i, span):
        pltpu.make_async_remote_copy(
            src_ref=part.at[span, :], dst_ref=theirs.at[span, :],
            send_sem=send_sem.at[i], recv_sem=recv_sem.at[i],
            device_id=(space, other), device_id_type=MESH,
        ).wait_recv()

    load.wait()
    face_mine, ghost_mine = pl.ds(face_at + mine, half), pl.ds(ghost_at + mine, half)
    face_other, ghost_other = pl.ds(face_at + not_mine, half), pl.ds(ghost_at + not_mine, half)
    here, there = pl.ds(mine, half), pl.ds(not_mine, half)
    arrived(0, face_mine)
    down_send[...] = own[face_mine, :] + theirs[face_mine, :]
    arrived(1, ghost_mine)
    up_send[...] = own[ghost_mine, :] + theirs[ghost_mine, :]
    sides = []
    for i, (src, dst, place) in enumerate(
        ((up_send, from_below, above), (down_send, from_above, below))
    ):
        side = pltpu.make_async_remote_copy(
            src_ref=src, dst_ref=dst.at[here, :],
            send_sem=side_send.at[i], recv_sem=side_recv.at[i],
            device_id=(place, state), device_id_type=MESH,
        )
        side.start()
        sides.append(side)

    gain, damp, center = coef[0], coef[1], coef[2]

    def step(h, now, before):
        return (h - center * now) * gain - damp * before

    stores = []

    def keep(src, dst, span):
        copy = pltpu.make_async_copy(
            src.at[span, :], dst.at[span, :], store_sem.at[len(stores)]
        )
        copy.start()
        stores.append(copy)

    for i in range(pieces):
        span = spans[i + 2]
        swaps[i + 2].wait_recv()
        new[span, :] = step(own[span, :] + theirs[span, :], cur[span, :], prev[span, :])
        keep(new, out, span)
    arrived(6, face_other)
    arrived(7, ghost_other)
    relays = []
    for i, dst in enumerate((from_below, from_above)):
        sides[i].wait_recv()
        relay = pltpu.make_async_remote_copy(
            src_ref=dst.at[here, :], dst_ref=dst.at[here, :],
            send_sem=relay_send.at[i], recv_sem=relay_recv.at[i],
            device_id=(space, other), device_id_type=MESH,
        )
        relay.start()
        relays.append(relay)

    def finish(face_span, ghost_span, span):
        h = own[face_span, :] + theirs[face_span, :]
        extra = from_below[span, :]
        h = h + jnp.where(space == 0, jnp.zeros_like(extra), extra)
        new[face_span, :] = step(h, cur[face_span, :], prev[face_span, :])
        keep(new, out, face_span)
        h = own[ghost_span, :] + theirs[ghost_span, :] + from_above[span, :]
        h = jnp.where(space == parts - 1, jnp.zeros_like(h), h)
        new_ghost[span, :] = step(h, cur_ghost[span, :], prev_ghost[span, :])
        keep(new_ghost, out_ghost, span)

    finish(face_mine, ghost_mine, here)
    for i, dst in enumerate((from_below, from_above)):
        pltpu.make_async_remote_copy(
            src_ref=dst.at[there, :], dst_ref=dst.at[there, :],
            send_sem=relay_send.at[i], recv_sem=relay_recv.at[i],
            device_id=(space, other), device_id_type=MESH,
        ).wait_recv()
    finish(face_other, ghost_other, there)
    for copy in swaps + sides + relays:
        copy.wait_send()
    for copy in stores:
        copy.wait()


def exchange(coef, part, cur, cur_ghost, prev, prev_ghost, qmain):
    qface = cur_ghost.shape[0]
    parts = lax.axis_size("space")
    vmem = pl.BlockSpec(memory_space=pltpu.VMEM)
    hbm = pl.BlockSpec(memory_space=pltpu.HBM)
    half = qface // 2
    return pl.pallas_call(
        functools.partial(exchange_kernel, qmain, qface, parts),
        name="exchange_update",
        out_shape=[
            jax.ShapeDtypeStruct(cur.shape, F32),
            jax.ShapeDtypeStruct(cur_ghost.shape, F32),
        ],
        in_specs=[pl.BlockSpec(memory_space=pltpu.SMEM), hbm] + [vmem] * 4,
        out_specs=[hbm, hbm],
        scratch_shapes=[
            pltpu.VMEM(part.shape, F32),
            pltpu.VMEM(part.shape, F32),
            pltpu.VMEM(cur.shape, F32),
            pltpu.VMEM(cur_ghost.shape, F32),
            pltpu.VMEM((half, LANES), F32),
            pltpu.VMEM((half, LANES), F32),
            pltpu.VMEM((qface, LANES), F32),
            pltpu.VMEM((qface, LANES), F32),
            pltpu.SemaphoreType.DMA,
            pltpu.SemaphoreType.DMA((8,)),
            pltpu.SemaphoreType.DMA((8,)),
            pltpu.SemaphoreType.DMA((8,)),
            pltpu.SemaphoreType.DMA((2,)),
            pltpu.SemaphoreType.DMA((2,)),
            pltpu.SemaphoreType.DMA((2,)),
            pltpu.SemaphoreType.DMA((2,)),
        ],
        compiler_params=pltpu.CompilerParams(
            collective_id=0, has_side_effects=True, vmem_limit_bytes=32 * 2**20
        ),
    )(coef, part, cur, cur_ghost, prev, prev_ghost)


def margin_kernel(grid, node_total, rounded, out, blocks, gram, sums, across, along, *sems):
    depth, width, ring = grid
    space, state = lax.axis_index("space"), lax.axis_index("state")
    z, x = space // width, lax.rem(space, width)
    y, core = state // 2, lax.rem(state, 2)
    chips = ring // 2
    state_send, state_recv, row_send, row_recv, x_send, x_recv, z_send, z_recv = sems
    friends = [(space, lax.rem(state + k, ring)) for k in range(1, ring)]
    x_friends = [(z * width + lax.rem(x + k, width), state) for k in range(1, width)]
    z_friends = [(lax.rem(z + k, depth) * width + x, state) for k in range(1, depth)]
    barrier = pltpu.get_barrier_semaphore()
    everyone = friends + x_friends + z_friends
    for device in everyone:
        pl.semaphore_signal(barrier, inc=1, device_id=device, device_id_type=MESH)
    pl.semaphore_wait(barrier, len(everyone))

    copies = []
    for k in range(1, chips):
        to = lax.rem(y + k, chips)
        copy = pltpu.make_async_remote_copy(
            src_ref=rounded.at[to], dst_ref=blocks.at[k],
            send_sem=state_send.at[k], recv_sem=state_recv.at[k],
            device_id=(space, 2 * to + core), device_id_type=MESH,
        )
        copy.start()
        copies.append(copy)
    blocks[0] = rounded[y]
    for copy in copies:
        copy.wait()
    ordered = jnp.concatenate([blocks[lax.rem(y + chips - i, chips)] for i in range(chips)], axis=0)
    gram[:, : ordered.shape[0]] = lax.dot_general(
        ordered, ordered, (((1,), (1,)), ((), ())), preferred_element_type=F32
    )
    gram[:, ordered.shape[0] :] = jnp.zeros_like(gram[:, ordered.shape[0] :])

    def add_up(sources, friends, slots, send, recv):
        copies = []
        for k, (src, device) in enumerate(zip(sources, friends), 1):
            copy = pltpu.make_async_remote_copy(
                src_ref=src, dst_ref=slots.at[k], send_sem=send.at[k], recv_sem=recv.at[k],
                device_id=device, device_id_type=MESH,
            )
            copy.start()
            copies.append(copy)
        for copy in copies:
            copy.wait()
        return functools.reduce(lambda a, b: a + b, [slots[k] for k in range(1, len(friends) + 1)])

    def rows_of(member):
        return pl.ds(pl.multiple_of(member * 8, 8), 8)

    rows = [gram.at[rows_of(device[1]), :] for device in friends]
    total = gram[rows_of(state), :] + add_up(rows, friends, sums, row_send, row_recv)
    across[0] = total
    total = total + add_up([across.at[0]] * (width - 1), x_friends, across, x_send, x_recv)
    along[0] = total
    total = total + add_up([along.at[0]] * (depth - 1), z_friends, along, z_send, z_recv)
    out[...] = total[:, : out.shape[1]] * (1.0 / node_total)


def margin_of(rounded, node_total):
    ring = lax.axis_size("state")
    parts = lax.axis_size("space")
    width = 4
    depth = parts // width
    chips = ring // 2
    count = 8 * ring
    vmem = pl.BlockSpec(memory_space=pltpu.VMEM)
    sems = [pltpu.SemaphoreType.DMA((n,)) for n in (chips, chips, ring, ring, width, width, depth, depth)]
    return pl.pallas_call(
        functools.partial(margin_kernel, (depth, width, ring), node_total),
        name="margin_rows",
        out_shape=jax.ShapeDtypeStruct((8, count), F32),
        in_specs=[vmem],
        out_specs=vmem,
        scratch_shapes=[
            pltpu.VMEM(rounded.shape, BF16),
            pltpu.VMEM((count, LANES), F32),
            pltpu.VMEM((ring, 8, LANES), F32),
            pltpu.VMEM((width, 8, LANES), F32),
            pltpu.VMEM((depth, 8, LANES), F32),
        ]
        + sems,
        compiler_params=pltpu.CompilerParams(
            collective_id=1, has_side_effects=True, vmem_limit_bytes=32 * 2**20
        ),
    )(rounded)


def final_kernel(qmain, qface, core_ref, mainface, face_hbm, emat, out, rounded, X, R, sems, *faces):
    copies = start_lists(face_hbm, faces, sems)
    expand_section(mainface, 0, X, 0, qmain, emat)
    expand_section(mainface, qmain, R, 0, qface, emat)
    for copy in copies:
        copy.wait()

    def put(q, carry):
        for j in range(G):
            X[pl.ds(faces[j][q], 1), :] = R[pl.ds(j * qface + q, 1), :]
        return carry

    lax.fori_loop(0, qface, put, 0, unroll=4)
    core = core_ref[0]

    def turn(i, carry):
        q = pl.multiple_of(i * 128, 128)
        rows = merge_groups([X[pl.ds(j * qmain + q, 128), :] for j in range(G)]).T
        for j in range(G):
            a = rows[j * W : j * W + 8]
            b = rows[j * W + 8 : j * W + 16]
            out[:, pl.ds(j * qmain + q, 128)] = jnp.where(core == 0, a, b)
        far = G // 2
        for j in range(far):
            a = rows[j * W : (j + 1) * W]
            b = rows[(far + j) * W : (far + j + 1) * W]
            rounded[j, :, pl.ds(q, 128)] = jnp.where(core == 0, a, b).astype(BF16)
        return carry

    lax.fori_loop(0, qmain // 128, turn, 0)


def final(core, mainface, face_nodes, emat, qmain):
    qface = mainface.shape[0] - qmain
    vmem = pl.BlockSpec(memory_space=pltpu.VMEM)
    return pl.pallas_call(
        functools.partial(final_kernel, qmain, qface),
        name="final_block",
        out_shape=[
            jax.ShapeDtypeStruct((8, G * qmain), F32),
            jax.ShapeDtypeStruct((G // 2, W, qmain), BF16),
        ],
        in_specs=[
            pl.BlockSpec(memory_space=pltpu.SMEM), vmem, pl.BlockSpec(memory_space=pl.ANY), vmem
        ],
        out_specs=[vmem, vmem],
        scratch_shapes=[
            pltpu.VMEM((G * qmain, LANES), F32),
            pltpu.VMEM((G * qface, LANES), F32),
            pltpu.SemaphoreType.DMA((G,)),
        ]
        + [pltpu.SMEM((qface,), jnp.int32)] * G,
        compiler_params=pltpu.CompilerParams(vmem_limit_bytes=VMEM_LIMIT),
    )(core, mainface, face_nodes.reshape(G, qface), emat)


def body(states, bounds, element_matrix, elem_nodes, face_nodes, kinetic, potential, elem_count):
    parts = lax.axis_size("space")
    members = lax.axis_size("state")
    core = lax.rem(lax.axis_index("state"), 2)
    npe, slot_count = elem_nodes.shape
    half = slot_count // 2
    chunks = half // G
    steps = npe // KU
    qmain = states.shape[1] // G

    alive = (jnp.arange(slot_count, dtype=jnp.int32) < elem_count[0]).astype(F32)

    def lanes_of(scale):
        mine = lax.dynamic_slice(scale, (core * half,), (half,))
        return jnp.repeat(mine.reshape(G, chunks).T, W, axis=1)

    kin = lanes_of(0.5 * kinetic * alive)
    pot = lanes_of(potential * alive)
    mine = lax.dynamic_slice(elem_nodes, (0, core * half), (npe, half))
    raw = mine.reshape(KU, steps, G, chunks).transpose(0, 2, 3, 1).reshape(KU * G, chunks * steps)
    raw = jnp.pad(raw, ((0, 0), (0, (-raw.shape[1]) % 128)))
    matrix = jnp.pad(element_matrix.reshape(2, npe, npe), ((0, 0), (0, 128 - npe), (0, 128 - npe)))
    matrix = matrix.reshape(256, 128)
    high = lax.reduce_precision(matrix, 8, 7)
    low = matrix - high
    mcat = jnp.concatenate([high, low, high], axis=1).astype(BF16)
    emat, fmat = expand_matrix(), fold_matrix()

    lowest, lower, upper = bounds[0], bounds[1], bounds[2]
    half_width = (upper - lower) / 2.0
    center = (upper + lower) / 2.0
    sigma = half_width / (lowest - center)
    gamma = 2.0 / sigma
    coefs = [jnp.stack([sigma / half_width, jnp.zeros_like(sigma), center])]
    for _ in range(DEG - 1):
        following = 1.0 / (gamma - sigma)
        coefs.append(jnp.stack([2.0 * following / half_width, sigma * following, center]))
        sigma = following

    partner = lax.ppermute(states, "state", [(i, i ^ 1) for i in range(members)])
    first = jnp.where(core == 0, states, partner)
    second = jnp.where(core == 0, partner, states)
    cur, face_send, slots = setup(first, second, face_nodes, raw, emat)
    ghost = lax.ppermute(face_send, "space", [(i, i - 1) for i in range(1, parts)]).astype(F32)
    prev, prev_ghost = cur, ghost
    for k in range(DEG):
        part = elements(cur, ghost, slots, mcat, kin, pot, emat, fmat, qmain, steps)
        new, new_ghost = exchange(coefs[k], part, cur, ghost, prev, prev_ghost, qmain)
        prev, prev_ghost, cur, ghost = cur, ghost, new, new_ghost
    filtered, rounded = final(core.reshape(1), cur, face_nodes, emat, qmain)
    margin = margin_of(rounded, states.shape[1] * parts)
    return filtered, margin


def solution(mesh):
    in_specs = (
        P("state", "space"),
        P(),
        P(),
        P(None, "space"),
        P("space"),
        P("space"),
        P("space"),
        P("space"),
    )
    out_specs = (P("state", "space"), P("state", None))
    return jax.shard_map(body, mesh=mesh, in_specs=in_specs, out_specs=out_specs, check_vma=False)
```

```python
import functools

import jax
import jax.numpy as jnp
import numpy as np
from jax import lax
from jax.experimental import pallas as pl
from jax.experimental.pallas import tpu as pltpu
from jax.sharding import PartitionSpec as P

DEG = 4
G = 8
W = 16
LANES = G * W
FACE_LIST = 1024
KU = 5
MESH = pl.DeviceIdType.MESH
F32 = jnp.float32
BF16 = jnp.bfloat16
VMEM_LIMIT = 58 * 2**20


def expand_matrix():
    l = np.arange(LANES)[:, None]
    m = np.arange(G * LANES)[None, :]
    one = (l // W == m // LANES) & (l % W == m % W)
    return jnp.asarray(np.concatenate([one, one], 0), BF16)


def fold_matrix():
    j = np.arange(G)[:, None, None, None]
    l = np.arange(LANES)[None, None, :, None]
    m = np.arange(LANES)[None, None, None, :]
    one = (m // W == j) & (m % W == l % W)
    one = np.broadcast_to(one, (G, 2, LANES, LANES))
    return jnp.asarray(one.reshape(G * 2 * LANES, LANES), BF16)


def split(value):
    high = value.astype(BF16)
    low = (value - high.astype(F32)).astype(BF16)
    return high, low


def lane_group(rows=1):
    return lax.broadcasted_iota(jnp.int32, (rows, LANES), 1) // W


def odd_groups(rows, step):
    return (lane_group(rows) & step) != 0


def merge_groups(rows):
    step = 1
    while len(rows) > 1:
        odd = odd_groups(rows[0].shape[0], step)
        rows = [jnp.where(odd, rows[a + 1], rows[a]) for a in range(0, len(rows), 2)]
        step *= 2
    return rows[0]


def expand_section(src, src_at, dst, dst_at, count, emat, block=512, also=None):
    block = min(block, count)

    def step(i, carry):
        q = pl.multiple_of(i * block, block)
        high, low = split(src[pl.ds(src_at + q, block), :])
        wide = jnp.dot(
            jnp.concatenate([high, low], axis=1), emat[...], preferred_element_type=F32
        )
        for j in range(G):
            dst[pl.ds(dst_at + j * count + q, block), :] = wide[:, j * LANES : (j + 1) * LANES]
        if also is not None:
            also(dst_at + i * block * G, block * G)
        return carry

    lax.fori_loop(0, count // block, step, 0)


def start_lists(source, lists, sems):
    copies = [
        pltpu.make_async_copy(source.at[k], lists[k], sems.at[k]) for k in range(len(lists))
    ]
    for copy in copies:
        copy.start()
    return copies


def start_faces(source, lists, sems):
    size = lists[0].shape[0]
    copies = [
        pltpu.make_async_copy(source.at[pl.ds(k * size, size)], lists[k], sems.at[k])
        for k in range(len(lists))
    ]
    for copy in copies:
        copy.start()
    return copies


def faces_at(lists, count, q):
    inside = lists[0].shape[0] // count
    spots = [q + i * count for i in range(inside)]
    return [lists[j // inside][spots[j % inside]] for j in range(G)]


def setup_kernel(
    nmain, nface, first, second, face_row, face_hbm, raw, emat, out, face_high, face_low, slots, X, sems, *faces
):
    qmain, qface = nmain // G, nface // G
    copies = start_faces(face_hbm, faces, sems)
    hi_count = nmain // 128
    chunk = 1024
    table = jnp.zeros((256, hi_count), F32)
    for at in range(0, nface, chunk):
        node = jnp.concatenate(
            [face_row[r : r + 1, :] for r in range(at // 128, (at + chunk) // 128)], axis=1
        )
        pos = lax.broadcasted_iota(jnp.int32, (1, chunk), 1) + (at + 1)
        low = lax.broadcasted_iota(jnp.int32, (128, chunk), 0) == (node & 127)
        high = lax.broadcasted_iota(jnp.int32, (hi_count, chunk), 0) == (node >> 7)
        big = jnp.where(low, (pos >> 6).astype(F32), 0.0)
        small = jnp.where(low, (pos & 63).astype(F32), 0.0)
        table += lax.dot_general(
            jnp.concatenate([big, small], axis=0).astype(BF16),
            high.astype(F32).astype(BF16),
            (((1,), (1,)), ((), ())),
            preferred_element_type=F32,
        )
    table = table.astype(BF16)
    width = raw.shape[1]
    owned = (KU - 1) * G
    for k in range(owned):
        node = raw[k : k + 1, :]
        high = lax.broadcasted_iota(jnp.int32, (hi_count, width), 0) == (node >> 7)
        got = jnp.dot(table, high.astype(F32).astype(BF16), preferred_element_type=F32)
        both = got[:128] * 64.0 + got[128:]
        low = lax.broadcasted_iota(jnp.int32, (128, width), 0) == (node & 127)
        pos = jnp.sum(jnp.where(low, both, 0.0), axis=0, keepdims=True).astype(jnp.int32)
        slots[k : k + 1, :] = jnp.where(pos > 0, nmain + pos - 1, node)
    slots[owned:, :] = raw[owned:, :] + nface
    def turn(i, carry):
        q = pl.multiple_of(i * 128, 128)
        parts = []
        for j in range(G):
            parts.append(first[:, pl.ds(j * qmain + q, 128)])
            parts.append(second[:, pl.ds(j * qmain + q, 128)])
        out[pl.ds(q, 128), :] = jnp.concatenate(parts, axis=0).T
        return carry

    lax.fori_loop(0, qmain // 128, turn, 0)
    expand_section(out, 0, X, 0, qmain, emat)
    for copy in copies:
        copy.wait()
    zero = jnp.zeros((1, LANES), F32)

    def take(q, carry):
        nodes = faces_at(faces, qface, q)
        out[pl.ds(qmain + q, 1), :] = merge_groups([X[pl.ds(n, 1), :] for n in nodes])
        for n in nodes:
            X[pl.ds(n, 1), :] = zero
        return carry

    lax.fori_loop(0, qface, take, 0, unroll=4)

    def pack(i, carry):
        q = pl.multiple_of(i * 8, 8)
        out[pl.ds(q, 8), :] = merge_groups([X[pl.ds(j * qmain + q, 8), :] for j in range(G)])
        return carry

    lax.fori_loop(0, qmain // 8, pack, 0, unroll=4)
    face_high[...], face_low[...] = split(out[qmain : qmain + qface, :])


def setup(first, second, face_nodes, raw, emat):
    nmain, nface = first.shape[1], face_nodes.shape[0]
    qmain, qface = nmain // G, nface // G
    vmem = pl.BlockSpec(memory_space=pltpu.VMEM)
    return pl.pallas_call(
        functools.partial(setup_kernel, nmain, nface),
        name="setup_rows",
        out_shape=[
            jax.ShapeDtypeStruct((qmain + qface, LANES), F32),
            jax.ShapeDtypeStruct((qface, LANES), BF16),
            jax.ShapeDtypeStruct((qface, LANES), BF16),
            jax.ShapeDtypeStruct(raw.shape, jnp.int32),
        ],
        in_specs=[vmem, vmem, vmem, pl.BlockSpec(memory_space=pl.ANY), vmem, vmem],
        out_specs=[vmem, vmem, vmem, vmem],
        scratch_shapes=[
            pltpu.VMEM((nmain, LANES), F32),
            pltpu.SemaphoreType.DMA((G * qface // FACE_LIST,)),
        ]
        + [pltpu.SMEM((FACE_LIST,), jnp.int32)] * (G * qface // FACE_LIST),
        compiler_params=pltpu.CompilerParams(vmem_limit_bytes=VMEM_LIMIT),
    )(first, second, face_nodes.reshape(nface // 128, 128), face_nodes, raw, emat)


def element_kernel(
    sections, chunks, steps, mainface, ghost, slots_hbm, mcat, kin, pot, emat, fmat,
    part, X, acc0, acc1, U, Y, sems, *lists,
):
    copies = start_lists(slots_hbm, lists, sems)
    accs = (acc0, acc1)

    def clear(row, count):
        row = pl.multiple_of(row, count)
        zero = jnp.zeros((count, LANES), F32)
        acc0[pl.ds(row, count), :] = zero
        acc1[pl.ds(row, count), :] = zero

    at = 0
    src, src_at = mainface, 0
    for i, count in enumerate(sections):
        if i == 2:
            src, src_at = ghost, 0
        expand_section(src, src_at, X, at, count, emat, also=clear)
        at += G * count
        src_at += count
    U[:, U.shape[1] - 8 :, :] = jnp.zeros((2, 8, LANES), F32)
    for copy in copies:
        copy.wait()
    group = lane_group()
    masks = [group == j for j in range(G)]

    def gather(c, half, r):
        t = (2 * c + half) * steps + r
        for b in range(KU):
            rows = [X[pl.ds(lists[b * G + j][t], 1), :] for j in range(G)]
            U[half, pl.ds(b * steps + r, 1), :] = merge_groups(rows)

    def scatter(c, half, r):
        t = (2 * c + half) * steps + r
        for b in range(KU):
            acc = accs[b % 2]
            y = Y[half, pl.ds(b * steps + r, 1), :]
            nodes = [lists[b * G + j][t] for j in range(G)]
            sums = [acc[pl.ds(n, 1), :] + y for n in nodes]
            for j in range(G):
                pltpu.store(acc.at[pl.ds(nodes[j], 1), :], sums[j], mask=masks[j])

    def product(c):
        high, low = split(jnp.concatenate([U[0], U[1]], axis=1))
        prod = jnp.dot(
            mcat[...], jnp.concatenate([high, high, low], axis=0), preferred_element_type=F32
        )
        for half in range(2):
            lanes = slice(half * LANES, (half + 1) * LANES)
            row = pl.ds(2 * c + half, 1)
            Y[half] = kin[row, :] * prod[:128, lanes] + pot[row, :] * prod[128:, lanes]

    def loop(*works):
        def step(r, carry):
            for half in range(2):
                for work, c in works:
                    work(c, half, r)
            return carry

        lax.fori_loop(0, steps, step, 0, unroll=KU)

    loop((gather, 0))

    def chunk(c, carry):
        product(c)
        loop((gather, c + 1), (scatter, c))
        return carry

    pairs = chunks // 2
    lax.fori_loop(0, pairs - 1, chunk, 0)
    product(pairs - 1)
    loop((scatter, pairs - 1))
    at, out_at = 0, 0
    for count in sections:
        block = min(count, 512)

        def fold(i, carry, at=at, out_at=out_at, count=count, block=block):
            q = pl.multiple_of(i * block, block)
            pieces = []
            for j in range(G):
                rows = pl.ds(at + j * count + q, block)
                pieces.extend(split(acc0[rows, :] + acc1[rows, :]))
            part[pl.ds(out_at + q, block), :] = jnp.dot(
                jnp.concatenate(pieces, axis=1), fmat[...], preferred_element_type=F32
            )
            return carry

        lax.fori_loop(0, count // block, fold, 0)
        at += G * count
        out_at += count


def elements(mainface, ghost, slots, mcat, kin, pot, emat, fmat, qmain, steps):
    qface = mainface.shape[0] - qmain
    sections = (qmain, qface, ghost.shape[0])
    total = sum(sections)
    chunks = kin.shape[0]
    vmem = pl.BlockSpec(memory_space=pltpu.VMEM)
    return pl.pallas_call(
        functools.partial(element_kernel, sections, chunks, steps),
        name="element_rows",
        out_shape=jax.ShapeDtypeStruct((total, LANES), F32),
        in_specs=[vmem, vmem, pl.BlockSpec(memory_space=pl.ANY)] + [vmem] * 5,
        out_specs=vmem,
        scratch_shapes=[pltpu.VMEM((G * total, LANES), F32)] * 3
        + [pltpu.VMEM((2, 128, LANES), F32)] * 2
        + [pltpu.SemaphoreType.DMA((KU * G,))]
        + [pltpu.SMEM((slots.shape[1],), jnp.int32)] * (KU * G),
        compiler_params=pltpu.CompilerParams(vmem_limit_bytes=VMEM_LIMIT),
    )(mainface, ghost, slots, mcat, kin, pot, emat, fmat)


def exchange_kernel(
    qmain, qface, parts, coef, part, cur_in, cur_ghost_in, prev_in, prev_ghost_in, out, out_ghost,
    own, cur, cur_ghost, prev, prev_ghost, theirs, new, new_ghost, up_send, down_send, from_below, from_above,
    load_sem, store_sem, send_sem, recv_sem, side_send, side_recv, relay_send, relay_recv,
):
    pieces = 4
    rows = qmain // pieces
    half = qface // 2
    space, state = lax.axis_index("space"), lax.axis_index("state")
    core = lax.rem(state, 2)
    other = state + 1 - 2 * core
    above = lax.rem(space + 1, parts)
    below = lax.rem(space + parts - 1, parts)
    loads = []
    for src, dst in (
        (part, own), (cur_in, cur), (prev_in, prev), (cur_ghost_in, cur_ghost), (prev_ghost_in, prev_ghost)
    ):
        load = pltpu.make_async_copy(src, dst, load_sem.at[len(loads)])
        load.start()
        loads.append(load)
    barrier = pltpu.get_barrier_semaphore()
    for device in ((space, other), (above, state), (below, state)):
        pl.semaphore_signal(barrier, inc=1, device_id=device, device_id_type=MESH)
    pl.semaphore_wait(barrier, 3)

    mine = pl.multiple_of(core * half, half)
    not_mine = pl.multiple_of((1 - core) * half, half)
    face_at, ghost_at = qmain, qmain + qface
    spans = (
        [pl.ds(face_at + not_mine, half), pl.ds(ghost_at + not_mine, half)]
        + [pl.ds(i * rows, rows) for i in range(pieces)]
        + [pl.ds(face_at + mine, half), pl.ds(ghost_at + mine, half)]
    )
    swaps = []
    for i, span in enumerate(spans):
        swap = pltpu.make_async_remote_copy(
            src_ref=part.at[span, :], dst_ref=theirs.at[span, :],
            send_sem=send_sem.at[i], recv_sem=recv_sem.at[i],
            device_id=(space, other), device_id_type=MESH,
        )
        swap.start()
        swaps.append(swap)

    def arrived(i, span):
        pltpu.make_async_remote_copy(
            src_ref=part.at[span, :], dst_ref=theirs.at[span, :],
            send_sem=send_sem.at[i], recv_sem=recv_sem.at[i],
            device_id=(space, other), device_id_type=MESH,
        ).wait_recv()

    for load in loads:
        load.wait()
    face_mine, ghost_mine = pl.ds(face_at + mine, half), pl.ds(ghost_at + mine, half)
    face_other, ghost_other = pl.ds(face_at + not_mine, half), pl.ds(ghost_at + not_mine, half)
    here, there = pl.ds(mine, half), pl.ds(not_mine, half)
    arrived(0, face_mine)
    down_send[...] = (own[face_mine, :] + theirs[face_mine, :]).astype(BF16)
    arrived(1, ghost_mine)
    up_send[...] = (own[ghost_mine, :] + theirs[ghost_mine, :]).astype(BF16)
    sides = []
    for i, (src, dst, place) in enumerate(
        ((up_send, from_below, above), (down_send, from_above, below))
    ):
        side = pltpu.make_async_remote_copy(
            src_ref=src, dst_ref=dst.at[here, :],
            send_sem=side_send.at[i], recv_sem=side_recv.at[i],
            device_id=(place, state), device_id_type=MESH,
        )
        side.start()
        sides.append(side)

    gain, damp, center = coef[0], coef[1], coef[2]

    def step(h, now, before):
        return (h - center * now) * gain - damp * before

    stores = []

    def keep(src, dst, span):
        copy = pltpu.make_async_copy(
            src.at[span, :], dst.at[span, :], store_sem.at[len(stores)]
        )
        copy.start()
        stores.append(copy)

    for i in range(pieces):
        span = spans[i + 2]
        swaps[i + 2].wait_recv()
        new[span, :] = step(own[span, :] + theirs[span, :], cur[span, :], prev[span, :])
        keep(new, out, span)
    arrived(6, face_other)
    arrived(7, ghost_other)
    relays = []
    for i, dst in enumerate((from_below, from_above)):
        sides[i].wait_recv()
        relay = pltpu.make_async_remote_copy(
            src_ref=dst.at[here, :], dst_ref=dst.at[here, :],
            send_sem=relay_send.at[i], recv_sem=relay_recv.at[i],
            device_id=(space, other), device_id_type=MESH,
        )
        relay.start()
        relays.append(relay)

    def finish(face_span, ghost_span, span):
        h = own[face_span, :] + theirs[face_span, :]
        extra = from_below[span, :].astype(F32)
        h = h + jnp.where(space == 0, jnp.zeros_like(extra), extra)
        new[face_span, :] = step(h, cur[face_span, :], prev[face_span, :])
        keep(new, out, face_span)
        h = own[ghost_span, :] + theirs[ghost_span, :] + from_above[span, :].astype(F32)
        h = jnp.where(space == parts - 1, jnp.zeros_like(h), h)
        new_ghost[span, :] = step(h, cur_ghost[span, :], prev_ghost[span, :])
        keep(new_ghost, out_ghost, span)

    finish(face_mine, ghost_mine, here)
    for i, dst in enumerate((from_below, from_above)):
        pltpu.make_async_remote_copy(
            src_ref=dst.at[there, :], dst_ref=dst.at[there, :],
            send_sem=relay_send.at[i], recv_sem=relay_recv.at[i],
            device_id=(space, other), device_id_type=MESH,
        ).wait_recv()
    finish(face_other, ghost_other, there)
    for copy in swaps + sides + relays:
        copy.wait_send()
    for copy in stores:
        copy.wait()


def exchange(coef, part, cur, cur_ghost, prev, prev_ghost, qmain):
    qface = cur_ghost.shape[0]
    parts = lax.axis_size("space")
    hbm = pl.BlockSpec(memory_space=pltpu.HBM)
    half = qface // 2
    return pl.pallas_call(
        functools.partial(exchange_kernel, qmain, qface, parts),
        name="exchange_update",
        out_shape=[
            jax.ShapeDtypeStruct(cur.shape, F32),
            jax.ShapeDtypeStruct(cur_ghost.shape, F32),
        ],
        in_specs=[pl.BlockSpec(memory_space=pltpu.SMEM)] + [hbm] * 5,
        out_specs=[hbm, hbm],
        scratch_shapes=[
            pltpu.VMEM(part.shape, F32),
            pltpu.VMEM(cur.shape, F32),
            pltpu.VMEM(cur_ghost.shape, F32),
            pltpu.VMEM(cur.shape, F32),
            pltpu.VMEM(cur_ghost.shape, F32),
            pltpu.VMEM(part.shape, F32),
            pltpu.VMEM(cur.shape, F32),
            pltpu.VMEM(cur_ghost.shape, F32),
            pltpu.VMEM((half, LANES), BF16),
            pltpu.VMEM((half, LANES), BF16),
            pltpu.VMEM((qface, LANES), BF16),
            pltpu.VMEM((qface, LANES), BF16),
            pltpu.SemaphoreType.DMA((5,)),
            pltpu.SemaphoreType.DMA((8,)),
            pltpu.SemaphoreType.DMA((8,)),
            pltpu.SemaphoreType.DMA((8,)),
            pltpu.SemaphoreType.DMA((2,)),
            pltpu.SemaphoreType.DMA((2,)),
            pltpu.SemaphoreType.DMA((2,)),
            pltpu.SemaphoreType.DMA((2,)),
        ],
        compiler_params=pltpu.CompilerParams(
            collective_id=0, has_side_effects=True, vmem_limit_bytes=VMEM_LIMIT
        ),
    )(coef, part, cur, cur_ghost, prev, prev_ghost)


def margin_kernel(grid, node_total, rounded, out, blocks, gram, sums, across, along, *sems):
    depth, width, ring = grid
    space, state = lax.axis_index("space"), lax.axis_index("state")
    z, x = space // width, lax.rem(space, width)
    y, core = state // 2, lax.rem(state, 2)
    chips = ring // 2
    state_send, state_recv, row_send, row_recv, x_send, x_recv, z_send, z_recv = sems
    friends = [(space, lax.rem(state + k, ring)) for k in range(1, ring)]
    x_friends = [(z * width + lax.rem(x + k, width), state) for k in range(1, width)]
    z_friends = [(lax.rem(z + k, depth) * width + x, state) for k in range(1, depth)]
    barrier = pltpu.get_barrier_semaphore()
    everyone = friends + x_friends + z_friends
    for device in everyone:
        pl.semaphore_signal(barrier, inc=1, device_id=device, device_id_type=MESH)
    pl.semaphore_wait(barrier, len(everyone))

    copies = []
    for k in range(1, chips):
        to = lax.rem(y + k, chips)
        copy = pltpu.make_async_remote_copy(
            src_ref=rounded.at[to], dst_ref=blocks.at[k],
            send_sem=state_send.at[k], recv_sem=state_recv.at[k],
            device_id=(space, 2 * to + core), device_id_type=MESH,
        )
        copy.start()
        copies.append(copy)
    blocks[0] = rounded[y]
    for copy in copies:
        copy.wait()
    ordered = jnp.concatenate([blocks[lax.rem(y + chips - i, chips)] for i in range(chips)], axis=0)
    gram[:, : ordered.shape[0]] = lax.dot_general(
        ordered, ordered, (((1,), (1,)), ((), ())), preferred_element_type=F32
    )
    gram[:, ordered.shape[0] :] = jnp.zeros_like(gram[:, ordered.shape[0] :])

    def add_up(sources, friends, slots, send, recv):
        copies = []
        for k, (src, device) in enumerate(zip(sources, friends), 1):
            copy = pltpu.make_async_remote_copy(
                src_ref=src, dst_ref=slots.at[k], send_sem=send.at[k], recv_sem=recv.at[k],
                device_id=device, device_id_type=MESH,
            )
            copy.start()
            copies.append(copy)
        for copy in copies:
            copy.wait()
        return functools.reduce(lambda a, b: a + b, [slots[k] for k in range(1, len(friends) + 1)])

    def rows_of(member):
        return pl.ds(pl.multiple_of(member * 8, 8), 8)

    rows = [gram.at[rows_of(device[1]), :] for device in friends]
    total = gram[rows_of(state), :] + add_up(rows, friends, sums, row_send, row_recv)
    across[0] = total
    total = total + add_up([across.at[0]] * (width - 1), x_friends, across, x_send, x_recv)
    along[0] = total
    total = total + add_up([along.at[0]] * (depth - 1), z_friends, along, z_send, z_recv)
    out[...] = total[:, : out.shape[1]] * (1.0 / node_total)


def margin_of(rounded, node_total):
    ring = lax.axis_size("state")
    parts = lax.axis_size("space")
    width = 4
    depth = parts // width
    chips = ring // 2
    count = 8 * ring
    vmem = pl.BlockSpec(memory_space=pltpu.VMEM)
    sems = [pltpu.SemaphoreType.DMA((n,)) for n in (chips, chips, ring, ring, width, width, depth, depth)]
    return pl.pallas_call(
        functools.partial(margin_kernel, (depth, width, ring), node_total),
        name="margin_rows",
        out_shape=jax.ShapeDtypeStruct((8, count), F32),
        in_specs=[vmem],
        out_specs=vmem,
        scratch_shapes=[
            pltpu.VMEM(rounded.shape, BF16),
            pltpu.VMEM((count, LANES), F32),
            pltpu.VMEM((ring, 8, LANES), F32),
            pltpu.VMEM((width, 8, LANES), F32),
            pltpu.VMEM((depth, 8, LANES), F32),
        ]
        + sems,
        compiler_params=pltpu.CompilerParams(
            collective_id=1, has_side_effects=True, vmem_limit_bytes=VMEM_LIMIT
        ),
    )(rounded)


def final_kernel(qmain, qface, core_ref, mainface, face_hbm, emat, out, rounded, X, R, sems, *faces):
    copies = start_faces(face_hbm, faces, sems)
    expand_section(mainface, 0, X, 0, qmain, emat)
    expand_section(mainface, qmain, R, 0, qface, emat)
    for copy in copies:
        copy.wait()

    def put(q, carry):
        for j, n in enumerate(faces_at(faces, qface, q)):
            X[pl.ds(n, 1), :] = R[pl.ds(j * qface + q, 1), :]
        return carry

    lax.fori_loop(0, qface, put, 0, unroll=4)
    core = core_ref[0]

    def turn(i, carry):
        q = pl.multiple_of(i * 128, 128)
        rows = merge_groups([X[pl.ds(j * qmain + q, 128), :] for j in range(G)]).T
        for j in range(G):
            a = rows[j * W : j * W + 8]
            b = rows[j * W + 8 : j * W + 16]
            out[:, pl.ds(j * qmain + q, 128)] = jnp.where(core == 0, a, b)
        far = G // 2
        for j in range(far):
            a = rows[j * W : (j + 1) * W]
            b = rows[(far + j) * W : (far + j + 1) * W]
            rounded[j, :, pl.ds(q, 128)] = jnp.where(core == 0, a, b).astype(BF16)
        return carry

    lax.fori_loop(0, qmain // 128, turn, 0)


def final(core, mainface, face_nodes, emat, qmain):
    qface = mainface.shape[0] - qmain
    vmem = pl.BlockSpec(memory_space=pltpu.VMEM)
    return pl.pallas_call(
        functools.partial(final_kernel, qmain, qface),
        name="final_block",
        out_shape=[
            jax.ShapeDtypeStruct((8, G * qmain), F32),
            jax.ShapeDtypeStruct((G // 2, W, qmain), BF16),
        ],
        in_specs=[
            pl.BlockSpec(memory_space=pltpu.SMEM), vmem, pl.BlockSpec(memory_space=pl.ANY), vmem
        ],
        out_specs=[vmem, vmem],
        scratch_shapes=[
            pltpu.VMEM((G * qmain, LANES), F32),
            pltpu.VMEM((G * qface, LANES), F32),
            pltpu.SemaphoreType.DMA((G * qface // FACE_LIST,)),
        ]
        + [pltpu.SMEM((FACE_LIST,), jnp.int32)] * (G * qface // FACE_LIST),
        compiler_params=pltpu.CompilerParams(vmem_limit_bytes=VMEM_LIMIT),
    )(core, mainface, face_nodes, emat)


def body(states, bounds, element_matrix, elem_nodes, face_nodes, kinetic, potential, elem_count):
    parts = lax.axis_size("space")
    members = lax.axis_size("state")
    core = lax.rem(lax.axis_index("state"), 2)
    npe, slot_count = elem_nodes.shape
    half = slot_count // 2
    chunks = half // G
    steps = npe // KU
    qmain = states.shape[1] // G

    alive = (jnp.arange(slot_count, dtype=jnp.int32) < elem_count[0]).astype(F32)

    def lanes_of(scale):
        mine = lax.dynamic_slice(scale, (core * half,), (half,))
        return jnp.repeat(mine.reshape(G, chunks).T, W, axis=1)

    kin = lanes_of(0.5 * kinetic * alive)
    pot = lanes_of(potential * alive)
    mine = lax.dynamic_slice(elem_nodes, (0, core * half), (npe, half))
    raw = mine.reshape(KU, steps, G, chunks).transpose(0, 2, 3, 1).reshape(KU * G, chunks * steps)
    raw = jnp.pad(raw, ((0, 0), (0, (-raw.shape[1]) % 128)))
    matrix = jnp.pad(element_matrix.reshape(2, npe, npe), ((0, 0), (0, 128 - npe), (0, 128 - npe)))
    matrix = matrix.reshape(256, 128)
    high = lax.reduce_precision(matrix, 8, 7)
    low = matrix - high
    mcat = jnp.concatenate([high, low, high], axis=1).astype(BF16)
    emat, fmat = expand_matrix(), fold_matrix()

    lowest, lower, upper = bounds[0], bounds[1], bounds[2]
    half_width = (upper - lower) / 2.0
    center = (upper + lower) / 2.0
    sigma = half_width / (lowest - center)
    gamma = 2.0 / sigma
    coefs = [jnp.stack([sigma / half_width, jnp.zeros_like(sigma), center])]
    for _ in range(DEG - 1):
        following = 1.0 / (gamma - sigma)
        coefs.append(jnp.stack([2.0 * following / half_width, sigma * following, center]))
        sigma = following

    partner = lax.ppermute(states, "state", [(i, i ^ 1) for i in range(members)])
    first = jnp.where(core == 0, states, partner)
    second = jnp.where(core == 0, partner, states)
    cur, face_high, face_low, slots = setup(first, second, face_nodes, raw, emat)
    downwards = [(i, i - 1) for i in range(1, parts)]
    ghost_high = lax.ppermute(face_high, "space", downwards).astype(F32)
    ghost_low = lax.ppermute(face_low, "space", downwards).astype(F32)
    prev, prev_ghost = cur, ghost_high + ghost_low
    for k in range(DEG):
        ghost = new_ghost if k else ghost_high
        part = elements(cur, ghost, slots, mcat, kin, pot, emat, fmat, qmain, steps)
        cur_ghost = ghost if k else prev_ghost
        new, new_ghost = exchange(coefs[k], part, cur, cur_ghost, prev, prev_ghost, qmain)
        prev, prev_ghost, cur = cur, cur_ghost, new
    filtered, rounded = final(core.reshape(1), cur, face_nodes, emat, qmain)
    margin = margin_of(rounded, states.shape[1] * parts)
    return filtered, margin


def solution(mesh):
    in_specs = (
        P("state", "space"),
        P(),
        P(),
        P(None, "space"),
        P("space"),
        P("space"),
        P("space"),
        P("space"),
    )
    out_specs = (P("state", "space"), P("state", None))
    return jax.shard_map(body, mesh=mesh, in_specs=in_specs, out_specs=out_specs, check_vma=False)
```

```python
import functools

import jax
import jax.numpy as jnp
import numpy as np
from jax import lax
from jax.experimental import pallas as pl
from jax.experimental.pallas import tpu as pltpu
from jax.sharding import PartitionSpec as P

DEG = 4
G = 8
W = 16
LANES = G * W
FACE_LIST = 1024
KU = 5
MESH = pl.DeviceIdType.MESH
F32 = jnp.float32
BF16 = jnp.bfloat16
VMEM_LIMIT = 58 * 2**20


def expand_matrix():
    l = np.arange(LANES)[:, None]
    m = np.arange(G * LANES)[None, :]
    one = (l // W == m // LANES) & (l % W == m % W)
    return jnp.asarray(np.concatenate([one, one], 0), BF16)


def fold_matrix():
    j = np.arange(G)[:, None, None, None]
    l = np.arange(LANES)[None, None, :, None]
    m = np.arange(LANES)[None, None, None, :]
    one = (m // W == j) & (m % W == l % W)
    one = np.broadcast_to(one, (G, 2, LANES, LANES))
    return jnp.asarray(one.reshape(G * 2 * LANES, LANES), BF16)


def split(value):
    high = value.astype(BF16)
    low = (value - high.astype(F32)).astype(BF16)
    return high, low


def lane_group(rows=1):
    return lax.broadcasted_iota(jnp.int32, (rows, LANES), 1) // W


def odd_groups(rows, step):
    return (lane_group(rows) & step) != 0


def merge_groups(rows):
    step = 1
    while len(rows) > 1:
        odd = odd_groups(rows[0].shape[0], step)
        rows = [jnp.where(odd, rows[a + 1], rows[a]) for a in range(0, len(rows), 2)]
        step *= 2
    return rows[0]


def expand_section(src, src_at, dst, dst_at, count, emat, block=512, also=None):
    block = min(block, count)

    def step(i, carry):
        q = pl.multiple_of(i * block, block)
        high, low = split(src[pl.ds(src_at + q, block), :])
        wide = jnp.dot(
            jnp.concatenate([high, low], axis=1), emat[...], preferred_element_type=F32
        )
        for j in range(G):
            dst[pl.ds(dst_at + j * count + q, block), :] = wide[:, j * LANES : (j + 1) * LANES]
        if also is not None:
            also(dst_at + i * block * G, block * G)
        return carry

    lax.fori_loop(0, count // block, step, 0)


def start_lists(source, lists, sems):
    copies = [
        pltpu.make_async_copy(source.at[k], lists[k], sems.at[k]) for k in range(len(lists))
    ]
    for copy in copies:
        copy.start()
    return copies


def start_faces(source, lists, sems):
    size = lists[0].shape[0]
    copies = [
        pltpu.make_async_copy(source.at[pl.ds(k * size, size)], lists[k], sems.at[k])
        for k in range(len(lists))
    ]
    for copy in copies:
        copy.start()
    return copies


def faces_at(lists, count, q):
    inside = lists[0].shape[0] // count
    spots = [q + i * count for i in range(inside)]
    return [lists[j // inside][spots[j % inside]] for j in range(G)]


def states_kernel(
    nmain, nface, core_ref, own, theirs, face_hbm, emat, out, face_high, face_low, X, sems, *faces
):
    qmain, qface = nmain // G, nface // G
    copies = start_faces(face_hbm, faces, sems)
    core = core_ref[0]

    def turn(i, carry):
        q = pl.multiple_of(i * 128, 128)
        parts = []
        for j in range(G):
            a = own[:, pl.ds(j * qmain + q, 128)]
            b = theirs[:, pl.ds(j * qmain + q, 128)]
            parts += [jnp.where(core == 0, a, b), jnp.where(core == 0, b, a)]
        out[pl.ds(q, 128), :] = jnp.concatenate(parts, axis=0).T
        return carry

    lax.fori_loop(0, qmain // 128, turn, 0, unroll=2)
    expand_section(out, 0, X, 0, qmain, emat)
    for copy in copies:
        copy.wait()
    zero = jnp.zeros((1, LANES), F32)

    def take(q, carry):
        nodes = faces_at(faces, qface, q)
        out[pl.ds(qmain + q, 1), :] = merge_groups([X[pl.ds(n, 1), :] for n in nodes])
        for n in nodes:
            X[pl.ds(n, 1), :] = zero
        return carry

    lax.fori_loop(0, qface, take, 0, unroll=8)

    def pack(i, carry):
        q = pl.multiple_of(i * 8, 8)
        out[pl.ds(q, 8), :] = merge_groups([X[pl.ds(j * qmain + q, 8), :] for j in range(G)])
        return carry

    lax.fori_loop(0, qmain // 8, pack, 0, unroll=4)
    face_high[...], face_low[...] = split(out[qmain : qmain + qface, :])


def states_rows(core, own, theirs, face_nodes, emat):
    nmain, nface = own.shape[1], face_nodes.shape[0]
    qmain, qface = nmain // G, nface // G
    vmem = pl.BlockSpec(memory_space=pltpu.VMEM)
    smem = pl.BlockSpec(memory_space=pltpu.SMEM)
    return pl.pallas_call(
        functools.partial(states_kernel, nmain, nface),
        name="states_rows",
        out_shape=[
            jax.ShapeDtypeStruct((qmain + qface, LANES), F32),
            jax.ShapeDtypeStruct((qface, LANES), BF16),
            jax.ShapeDtypeStruct((qface, LANES), BF16),
        ],
        in_specs=[smem, vmem, vmem, pl.BlockSpec(memory_space=pl.ANY), vmem],
        out_specs=[vmem, vmem, vmem],
        scratch_shapes=[
            pltpu.VMEM((nmain, LANES), F32),
            pltpu.SemaphoreType.DMA((nface // FACE_LIST,)),
        ]
        + [pltpu.SMEM((FACE_LIST,), jnp.int32)] * (nface // FACE_LIST),
        compiler_params=pltpu.CompilerParams(vmem_limit_bytes=VMEM_LIMIT),
    )(core, own, theirs, face_nodes, emat)


def prepare_kernel(
    nmain, nface, chunks, after, core_ref, count_ref, bounds, raw, face_rows, matrix, kinetic, potential,
    slots, scales, mcat, homes, *rest
):
    del after
    coefs, padded = rest[:DEG], rest[DEG]
    shape = (8, LANES)
    lowest, lower, upper = (jnp.full(shape, bounds[i], F32) for i in range(3))
    half_width = (upper - lower) / 2.0
    center = (upper + lower) / 2.0
    sigma = half_width / (lowest - center)
    gamma = 2.0 / sigma
    coefs[0][...] = jnp.concatenate([sigma / half_width, jnp.zeros(shape, F32), center], axis=0)
    for k in range(1, DEG):
        following = 1.0 / (gamma - sigma)
        coefs[k][...] = jnp.concatenate(
            [2.0 * following / half_width, sigma * following, center], axis=0
        )
        sigma = following
    core, count = core_ref[0], count_ref[0]
    place = lax.broadcasted_iota(jnp.int32, (1, LANES), 1)
    alive = (core * LANES + place) < count
    lane = lax.broadcasted_iota(jnp.int32, (chunks, LANES), 1)
    chunk = lax.broadcasted_iota(jnp.int32, (chunks, LANES), 0)
    spread = (
        lax.broadcasted_iota(jnp.int32, (LANES, LANES), 0) // chunks
        == lax.broadcasted_iota(jnp.int32, (LANES, LANES), 1) // W
    ).astype(F32)
    for i, (scale, factor) in enumerate(((kinetic, 0.5), (potential, 1.0))):
        row = jnp.where(core == 0, scale[0:1, :], scale[1:2, :]) * factor
        row = jnp.where(alive, row, 0.0)
        wide = jnp.where(lax.rem(lane, chunks) == chunk, row, 0.0)
        scales[i * chunks : (i + 1) * chunks, :] = jnp.dot(
            wide, spread, precision=lax.Precision.HIGHEST, preferred_element_type=F32
        )
    npe = matrix.shape[1]
    padded[...] = jnp.zeros_like(padded)
    padded[0:npe, 0:npe] = matrix[0:npe, :]
    padded[128 : 128 + npe, 0:npe] = matrix[npe : 2 * npe, :]
    high, low = split(padded[...])
    mcat[...] = jnp.concatenate([high, low, high], axis=1)
    hi_count = nmain // 128
    size = 1024
    table = jnp.zeros((256, hi_count), F32)
    for at in range(0, nface, size):
        node = jnp.concatenate(
            [face_rows[r : r + 1, :] for r in range(at // 128, (at + size) // 128)], axis=1
        )
        pos = lax.broadcasted_iota(jnp.int32, (1, size), 1) + (at + 1)
        low = lax.broadcasted_iota(jnp.int32, (128, size), 0) == (node & 127)
        high = lax.broadcasted_iota(jnp.int32, (hi_count, size), 0) == (node >> 7)
        big = jnp.where(low, (pos >> 6).astype(F32), 0.0)
        small = jnp.where(low, (pos & 63).astype(F32), 0.0)
        table += lax.dot_general(
            jnp.concatenate([big, small], axis=0).astype(BF16),
            high.astype(F32).astype(BF16),
            (((1,), (1,)), ((), ())),
            preferred_element_type=F32,
        )
    position = (table[:128] * 64.0 + table[128:]).T.astype(jnp.int32)
    node = (
        lax.broadcasted_iota(jnp.int32, (hi_count, 128), 0) * 128
        + lax.broadcasted_iota(jnp.int32, (hi_count, 128), 1)
    )
    homes[...] = jnp.where(position > 0, nmain + position - 1, node)
    table = table.astype(BF16)
    width = raw.shape[1]
    owned = (KU - 1) * G
    slots[...] = jnp.zeros_like(slots)
    for k in range(owned):
        node = raw[k : k + 1, :]
        high = lax.broadcasted_iota(jnp.int32, (hi_count, width), 0) == (node >> 7)
        got = jnp.dot(table, high.astype(F32).astype(BF16), preferred_element_type=F32)
        both = got[:128] * 64.0 + got[128:]
        low = lax.broadcasted_iota(jnp.int32, (128, width), 0) == (node & 127)
        pos = jnp.sum(jnp.where(low, both, 0.0), axis=0, keepdims=True).astype(jnp.int32)
        slots[k : k + 1, :width] = jnp.where(pos > 0, nmain + pos - 1, node)
    slots[owned:, :width] = raw[owned:, :] + nface


def prepare(after, core, count, bounds, raw, face_nodes, matrix, kinetic, potential, nmain, chunks):
    nface = face_nodes.shape[0]
    vmem = pl.BlockSpec(memory_space=pltpu.VMEM)
    smem = pl.BlockSpec(memory_space=pltpu.SMEM)
    width = -(-raw.shape[1] // 128) * 128
    return pl.pallas_call(
        functools.partial(prepare_kernel, nmain, nface, chunks),
        name="prepare_lists",
        out_shape=[
            jax.ShapeDtypeStruct((raw.shape[0], width), jnp.int32),
            jax.ShapeDtypeStruct((2 * chunks, LANES), F32),
            jax.ShapeDtypeStruct((256, 384), BF16),
            jax.ShapeDtypeStruct((nmain // 128, 128), jnp.int32),
        ]
        + [jax.ShapeDtypeStruct((24, LANES), F32)] * DEG,
        in_specs=[pl.BlockSpec(memory_space=pl.ANY)] + [smem] * 3 + [vmem] * 5,
        out_specs=[vmem] * (4 + DEG),
        scratch_shapes=[pltpu.VMEM((256, 128), F32)],
        compiler_params=pltpu.CompilerParams(vmem_limit_bytes=VMEM_LIMIT),
        cost_estimate=pl.CostEstimate(flops=10**9, bytes_accessed=2**24, transcendentals=0),
    )(
        after, core, count, bounds, raw, face_nodes.reshape(nface // 128, 128), matrix,
        kinetic.reshape(2, LANES), potential.reshape(2, LANES),
    )


def element_kernel(
    sections, chunks, steps, mainface, ghost, slots_hbm, mcat, scales, emat, fmat,
    part, X, acc0, acc1, U, Y, sems, *lists,
):
    copies = start_lists(slots_hbm, lists, sems)
    accs = (acc0, acc1)

    def clear(row, count):
        row = pl.multiple_of(row, count)
        acc0[pl.ds(row, count), :] = jnp.zeros((count, LANES), F32)

    at = 0
    src, src_at = mainface, 0
    for i, count in enumerate(sections):
        if i == 2:
            src, src_at = ghost, 0
        expand_section(src, src_at, X, at, count, emat, also=clear)
        at += G * count
        src_at += count
    U[:, U.shape[1] - 8 :, :] = jnp.zeros((2, 8, LANES), F32)
    for copy in copies:
        copy.wait()
    group = lane_group()
    masks = [group == j for j in range(G)]

    def gather(c, half, r):
        t = (2 * c + half) * steps + r
        for b in range(KU):
            rows = [X[pl.ds(lists[b * G + j][t], 1), :] for j in range(G)]
            U[half, pl.ds(b * steps + r, 1), :] = merge_groups(rows)

    def scatter(c, half, r):
        t = (2 * c + half) * steps + r
        for b in range(KU):
            acc = accs[b % 2]
            y = Y[half, pl.ds(b * steps + r, 1), :]
            nodes = [lists[b * G + j][t] for j in range(G)]
            sums = [acc[pl.ds(n, 1), :] + y for n in nodes]
            for j in range(G):
                pltpu.store(acc.at[pl.ds(nodes[j], 1), :], sums[j], mask=masks[j])

    def product(c):
        high, low = split(jnp.concatenate([U[0], U[1]], axis=1))
        prod = jnp.dot(
            mcat[...], jnp.concatenate([high, high, low], axis=0), preferred_element_type=F32
        )
        for half in range(2):
            lanes = slice(half * LANES, (half + 1) * LANES)
            kin = scales[pl.ds(2 * c + half, 1), :]
            pot = scales[pl.ds(chunks + 2 * c + half, 1), :]
            Y[half] = kin * prod[:128, lanes] + pot * prod[128:, lanes]

    def loop(*works):
        def step(r, carry):
            for half in range(2):
                for work, c in works:
                    work(c, half, r)
            return carry

        lax.fori_loop(0, steps, step, 0, unroll=KU)

    share = -(-acc1.shape[0] // (8 * steps)) * 8

    def wipe(c, half, r):
        if half == 0:
            start = pl.multiple_of(jnp.minimum(r * share, acc1.shape[0] - share), 8)
            acc1[pl.ds(start, share), :] = jnp.zeros((share, LANES), F32)

    loop((gather, 0), (wipe, 0))

    def chunk(c, carry):
        product(c)
        loop((gather, c + 1), (scatter, c))
        return carry

    pairs = chunks // 2
    lax.fori_loop(0, pairs - 1, chunk, 0)
    product(pairs - 1)
    loop((scatter, pairs - 1))
    at, out_at = 0, 0
    for count in sections:
        block = min(count, 512)

        def fold(i, carry, at=at, out_at=out_at, count=count, block=block):
            q = pl.multiple_of(i * block, block)
            pieces = []
            for j in range(G):
                rows = pl.ds(at + j * count + q, block)
                pieces.extend(split(acc0[rows, :] + acc1[rows, :]))
            part[pl.ds(out_at + q, block), :] = jnp.dot(
                jnp.concatenate(pieces, axis=1), fmat[...], preferred_element_type=F32
            )
            return carry

        lax.fori_loop(0, count // block, fold, 0)
        at += G * count
        out_at += count


def elements(mainface, ghost, slots, mcat, scales, emat, fmat, qmain, steps):
    qface = mainface.shape[0] - qmain
    sections = (qmain, qface, ghost.shape[0])
    total = sum(sections)
    chunks = scales.shape[0] // 2
    vmem = pl.BlockSpec(memory_space=pltpu.VMEM)
    return pl.pallas_call(
        functools.partial(element_kernel, sections, chunks, steps),
        name="element_rows",
        out_shape=jax.ShapeDtypeStruct((total, LANES), F32),
        in_specs=[vmem, vmem, pl.BlockSpec(memory_space=pl.ANY)] + [vmem] * 4,
        out_specs=vmem,
        scratch_shapes=[pltpu.VMEM((G * total, LANES), F32)] * 3
        + [pltpu.VMEM((2, 128, LANES), F32)] * 2
        + [pltpu.SemaphoreType.DMA((KU * G,))]
        + [pltpu.SMEM((slots.shape[1],), jnp.int32)] * (KU * G),
        compiler_params=pltpu.CompilerParams(vmem_limit_bytes=VMEM_LIMIT),
    )(mainface, ghost, slots, mcat, scales, emat, fmat)


def exchange_kernel(
    qmain, qface, parts, coef, part, cur_in, cur_ghost_in, prev_in, prev_ghost_in, out, out_ghost,
    own, cur, cur_ghost, prev, prev_ghost, theirs, new, new_ghost, up_send, down_send, from_below, from_above,
    load_sem, store_sem, send_sem, recv_sem, side_send, side_recv, relay_send, relay_recv,
):
    pieces = 4
    rows = qmain // pieces
    half = qface // 2
    space, state = lax.axis_index("space"), lax.axis_index("state")
    core = lax.rem(state, 2)
    other = state + 1 - 2 * core
    above = lax.rem(space + 1, parts)
    below = lax.rem(space + parts - 1, parts)
    loads = []
    for src, dst in (
        (part, own), (cur_in, cur), (prev_in, prev), (cur_ghost_in, cur_ghost), (prev_ghost_in, prev_ghost)
    ):
        load = pltpu.make_async_copy(src, dst, load_sem.at[len(loads)])
        load.start()
        loads.append(load)
    barrier = pltpu.get_barrier_semaphore()
    for device in ((space, other), (above, state), (below, state)):
        pl.semaphore_signal(barrier, inc=1, device_id=device, device_id_type=MESH)
    pl.semaphore_wait(barrier, 3)

    mine = pl.multiple_of(core * half, half)
    not_mine = pl.multiple_of((1 - core) * half, half)
    face_at, ghost_at = qmain, qmain + qface
    spans = (
        [pl.ds(face_at + not_mine, half), pl.ds(ghost_at + not_mine, half)]
        + [pl.ds(i * rows, rows) for i in range(pieces)]
        + [pl.ds(face_at + mine, half), pl.ds(ghost_at + mine, half)]
    )
    swaps = []
    for i, span in enumerate(spans):
        swap = pltpu.make_async_remote_copy(
            src_ref=part.at[span, :], dst_ref=theirs.at[span, :],
            send_sem=send_sem.at[i], recv_sem=recv_sem.at[i],
            device_id=(space, other), device_id_type=MESH,
        )
        swap.start()
        swaps.append(swap)

    def arrived(i, span):
        pltpu.make_async_remote_copy(
            src_ref=part.at[span, :], dst_ref=theirs.at[span, :],
            send_sem=send_sem.at[i], recv_sem=recv_sem.at[i],
            device_id=(space, other), device_id_type=MESH,
        ).wait_recv()

    loads[0].wait()
    face_mine, ghost_mine = pl.ds(face_at + mine, half), pl.ds(ghost_at + mine, half)
    face_other, ghost_other = pl.ds(face_at + not_mine, half), pl.ds(ghost_at + not_mine, half)
    here, there = pl.ds(mine, half), pl.ds(not_mine, half)
    arrived(0, face_mine)
    down_send[...] = (own[face_mine, :] + theirs[face_mine, :]).astype(BF16)
    arrived(1, ghost_mine)
    up_send[...] = (own[ghost_mine, :] + theirs[ghost_mine, :]).astype(BF16)
    sides = []
    for i, (src, dst, place) in enumerate(
        ((up_send, from_below, above), (down_send, from_above, below))
    ):
        side = pltpu.make_async_remote_copy(
            src_ref=src, dst_ref=dst.at[here, :],
            send_sem=side_send.at[i], recv_sem=side_recv.at[i],
            device_id=(place, state), device_id_type=MESH,
        )
        side.start()
        sides.append(side)

    for load in loads[1:]:
        load.wait()
    gain, damp, center = coef[0:1, :], coef[8:9, :], coef[16:17, :]

    def step(h, now, before):
        return (h - center * now) * gain - damp * before

    stores = []

    def keep(src, dst, span):
        copy = pltpu.make_async_copy(
            src.at[span, :], dst.at[span, :], store_sem.at[len(stores)]
        )
        copy.start()
        stores.append(copy)

    for i in range(pieces):
        span = spans[i + 2]
        swaps[i + 2].wait_recv()
        new[span, :] = step(own[span, :] + theirs[span, :], cur[span, :], prev[span, :])
        keep(new, out, span)
    arrived(6, face_other)
    arrived(7, ghost_other)
    relays = []
    for i, dst in enumerate((from_below, from_above)):
        sides[i].wait_recv()
        relay = pltpu.make_async_remote_copy(
            src_ref=dst.at[here, :], dst_ref=dst.at[here, :],
            send_sem=relay_send.at[i], recv_sem=relay_recv.at[i],
            device_id=(space, other), device_id_type=MESH,
        )
        relay.start()
        relays.append(relay)

    def finish(face_span, ghost_span, span):
        h = own[face_span, :] + theirs[face_span, :]
        extra = from_below[span, :].astype(F32)
        h = h + jnp.where(space == 0, jnp.zeros_like(extra), extra)
        new[face_span, :] = step(h, cur[face_span, :], prev[face_span, :])
        keep(new, out, face_span)
        h = own[ghost_span, :] + theirs[ghost_span, :] + from_above[span, :].astype(F32)
        h = jnp.where(space == parts - 1, jnp.zeros_like(h), h)
        new_ghost[span, :] = step(h, cur_ghost[span, :], prev_ghost[span, :])
        keep(new_ghost, out_ghost, span)

    finish(face_mine, ghost_mine, here)
    for i, dst in enumerate((from_below, from_above)):
        pltpu.make_async_remote_copy(
            src_ref=dst.at[there, :], dst_ref=dst.at[there, :],
            send_sem=relay_send.at[i], recv_sem=relay_recv.at[i],
            device_id=(space, other), device_id_type=MESH,
        ).wait_recv()
    finish(face_other, ghost_other, there)
    for copy in swaps + sides + relays:
        copy.wait_send()
    for copy in stores:
        copy.wait()


def exchange(coef, part, cur, cur_ghost, prev, prev_ghost, qmain):
    qface = cur_ghost.shape[0]
    parts = lax.axis_size("space")
    hbm = pl.BlockSpec(memory_space=pltpu.HBM)
    half = qface // 2
    return pl.pallas_call(
        functools.partial(exchange_kernel, qmain, qface, parts),
        name="exchange_update",
        out_shape=[
            jax.ShapeDtypeStruct(cur.shape, F32),
            jax.ShapeDtypeStruct(cur_ghost.shape, F32),
        ],
        in_specs=[pl.BlockSpec(memory_space=pltpu.VMEM)] + [hbm] * 5,
        out_specs=[hbm, hbm],
        scratch_shapes=[
            pltpu.VMEM(part.shape, F32),
            pltpu.VMEM(cur.shape, F32),
            pltpu.VMEM(cur_ghost.shape, F32),
            pltpu.VMEM(cur.shape, F32),
            pltpu.VMEM(cur_ghost.shape, F32),
            pltpu.VMEM(part.shape, F32),
            pltpu.VMEM(cur.shape, F32),
            pltpu.VMEM(cur_ghost.shape, F32),
            pltpu.VMEM((half, LANES), BF16),
            pltpu.VMEM((half, LANES), BF16),
            pltpu.VMEM((qface, LANES), BF16),
            pltpu.VMEM((qface, LANES), BF16),
            pltpu.SemaphoreType.DMA((5,)),
            pltpu.SemaphoreType.DMA((8,)),
            pltpu.SemaphoreType.DMA((8,)),
            pltpu.SemaphoreType.DMA((8,)),
            pltpu.SemaphoreType.DMA((2,)),
            pltpu.SemaphoreType.DMA((2,)),
            pltpu.SemaphoreType.DMA((2,)),
            pltpu.SemaphoreType.DMA((2,)),
        ],
        compiler_params=pltpu.CompilerParams(
            collective_id=0, has_side_effects=True, vmem_limit_bytes=VMEM_LIMIT
        ),
    )(coef, part, cur, cur_ghost, prev, prev_ghost)


def finish_kernel(
    grid, qmain, source, homes_hbm, emat, out, margin,
    face, X, C, rounded, blocks, gram, sums, across, along, load_sem, home_sems, *rest,
):
    sems, homes = rest[:8], rest[8:]
    depth, width, ring = grid
    space, state = lax.axis_index("space"), lax.axis_index("state")
    z, x = space // width, lax.rem(space, width)
    y, core = state // 2, lax.rem(state, 2)
    chips = ring // 2
    state_send, state_recv, row_send, row_recv, x_send, x_recv, z_send, z_recv = sems
    friends = [(space, lax.rem(state + k, ring)) for k in range(1, ring)]
    x_friends = [(z * width + lax.rem(x + k, width), state) for k in range(1, width)]
    z_friends = [(lax.rem(z + k, depth) * width + x, state) for k in range(1, depth)]
    load = pltpu.make_async_copy(source, face, load_sem)
    load.start()
    lists = start_faces(homes_hbm, homes, home_sems)
    barrier = pltpu.get_barrier_semaphore()
    everyone = friends + x_friends + z_friends
    for device in everyone:
        pl.semaphore_signal(barrier, inc=1, device_id=device, device_id_type=MESH)
    load.wait()
    share = rounded.shape[1]
    for i in range(ring):
        rounded[i] = face[i * share : (i + 1) * share, :].astype(BF16)
    pl.semaphore_wait(barrier, len(everyone))

    copies = []
    for k in range(1, chips):
        to = lax.rem(y + k, chips)
        copy = pltpu.make_async_remote_copy(
            src_ref=rounded.at[core * chips + to], dst_ref=blocks.at[k],
            send_sem=state_send.at[k], recv_sem=state_recv.at[k],
            device_id=(space, 2 * to + core), device_id_type=MESH,
        )
        copy.start()
        copies.append(copy)
    blocks[0] = rounded[core * chips + y]
    qface = source.shape[0] - qmain
    expand_section(face, 0, X, 0, qmain, emat)
    expand_section(face, qmain, X, G * qmain, qface, emat)
    for copy in lists:
        copy.wait()
    for copy in copies:
        copy.wait()

    def place(first, last):
        def block(i, carry):
            start = i * 128

            def row(q, inner):
                nodes = [homes[j][start + q] for j in range(G)]
                C[pl.ds(q, 1), :] = merge_groups([X[pl.ds(n, 1), :] for n in nodes])
                return inner

            lax.fori_loop(0, 128, row, 0, unroll=8)
            turned = C[...].T
            for j in range(G):
                a = turned[j * W : j * W + 8]
                b = turned[j * W + 8 : j * W + 16]
                columns = pl.ds(pl.multiple_of(j * qmain + start, 128), 128)
                out[:, columns] = jnp.where(core == 0, a, b)
            return carry

        lax.fori_loop(first, last, block, 0)

    wide = jnp.concatenate([blocks[lax.rem(y + chips - i, chips)] for i in range(chips)], axis=1)
    pairs = lax.dot_general(
        wide, wide, (((0,), (0,)), ((), ())), preferred_element_type=F32
    )
    lanes = chips * LANES
    group = lax.rem(lax.broadcasted_iota(jnp.int32, (W, lanes), 1), LANES) // W
    rows = []
    for i in range(chips):
        terms = [
            jnp.where(group == j, pairs[i * LANES + j * W : i * LANES + (j + 1) * W, :], 0.0)
            for j in range(G)
        ]
        rows.append(functools.reduce(lambda a, b: a + b, terms))
    lane = lax.broadcasted_iota(jnp.int32, (lanes, LANES), 0)
    column = lax.broadcasted_iota(jnp.int32, (lanes, LANES), 1)
    gather = (lane // LANES * W + lax.rem(lane, W) == column).astype(F32)
    gram[...] = jnp.dot(
        jnp.concatenate(rows, axis=0), gather,
        precision=lax.Precision.HIGHEST, preferred_element_type=F32,
    )

    def send(sources, friends, slots, send_sem, recv_sem):
        copies = []
        for k, (src, device) in enumerate(zip(sources, friends), 1):
            copy = pltpu.make_async_remote_copy(
                src_ref=src, dst_ref=slots.at[k], send_sem=send_sem.at[k], recv_sem=recv_sem.at[k],
                device_id=device, device_id_type=MESH,
            )
            copy.start()
            copies.append(copy)
        return copies

    def collect(copies, slots):
        for copy in copies:
            copy.wait()
        return functools.reduce(
            lambda a, b: a + b, [slots[k] for k in range(1, len(copies) + 1)]
        )

    def rows_of(member):
        return pl.ds(pl.multiple_of(member * 8, 8), 8)

    blocks_left = qmain // 128
    cut1, cut2 = blocks_left // 3, 2 * blocks_left // 3
    copies = send(
        [gram.at[rows_of(device[1]), :] for device in friends], friends, sums, row_send, row_recv
    )
    place(0, cut1)
    total = gram[rows_of(state), :] + collect(copies, sums)
    across[0] = total
    copies = send([across.at[0]] * (width - 1), x_friends, across, x_send, x_recv)
    place(cut1, cut2)
    total = total + collect(copies, across)
    along[0] = total
    copies = send([along.at[0]] * (depth - 1), z_friends, along, z_send, z_recv)
    place(cut2, blocks_left)
    total = total + collect(copies, along)
    margin[...] = total[:, : margin.shape[1]]


def finish(source, homes, emat, qmain):
    ring = lax.axis_size("state")
    parts = lax.axis_size("space")
    width = 4
    depth = parts // width
    chips = ring // 2
    count = 8 * ring
    total = source.shape[0]
    share = total // ring
    vmem = pl.BlockSpec(memory_space=pltpu.VMEM)
    anywhere = pl.BlockSpec(memory_space=pl.ANY)
    sems = [pltpu.SemaphoreType.DMA((n,)) for n in (chips, chips, ring, ring, width, width, depth, depth)]
    return pl.pallas_call(
        functools.partial(finish_kernel, (depth, width, ring), qmain),
        name="finish_block",
        out_shape=[
            jax.ShapeDtypeStruct((8, G * qmain), F32),
            jax.ShapeDtypeStruct((8, count), F32),
        ],
        in_specs=[anywhere, anywhere, vmem],
        out_specs=[vmem, vmem],
        scratch_shapes=[
            pltpu.VMEM(source.shape, F32),
            pltpu.VMEM((G * total, LANES), F32),
            pltpu.VMEM((128, LANES), F32),
            pltpu.VMEM((ring, share, LANES), BF16),
            pltpu.VMEM((chips, share, LANES), BF16),
            pltpu.VMEM((count, LANES), F32),
            pltpu.VMEM((ring, 8, LANES), F32),
            pltpu.VMEM((width, 8, LANES), F32),
            pltpu.VMEM((depth, 8, LANES), F32),
            pltpu.SemaphoreType.DMA,
            pltpu.SemaphoreType.DMA((G,)),
        ]
        + sems
        + [pltpu.SMEM((qmain,), jnp.int32)] * G,
        compiler_params=pltpu.CompilerParams(
            collective_id=1, has_side_effects=True, vmem_limit_bytes=VMEM_LIMIT
        ),
    )(source, homes, emat)


def body(states, bounds, element_matrix, elem_nodes, face_nodes, kinetic, potential, elem_count):
    parts = lax.axis_size("space")
    members = lax.axis_size("state")
    core = lax.rem(lax.axis_index("state"), 2)
    npe, slot_count = elem_nodes.shape
    half = slot_count // 2
    chunks = half // G
    steps = npe // KU
    qmain = states.shape[1] // G

    mine = lax.dynamic_slice(elem_nodes, (0, core * half), (npe, half))
    raw = mine.reshape(KU, steps, G, chunks).transpose(0, 2, 3, 1).reshape(KU * G, chunks * steps)
    emat, fmat = expand_matrix(), fold_matrix()
    which = core.reshape(1)

    partner = lax.ppermute(states, "state", [(i, i ^ 1) for i in range(members)])
    cur, face_high, face_low = states_rows(which, states, partner, face_nodes, emat)
    downwards = [(i, i - 1) for i in range(1, parts)]
    ghost_high = lax.ppermute(face_high, "space", downwards).astype(F32)
    ghost_low = lax.ppermute(face_low, "space", downwards).astype(F32)
    slots, scales, mcat, homes, *coefs = prepare(
        face_low, which, elem_count, bounds, raw, face_nodes, element_matrix, kinetic, potential,
        states.shape[1], chunks,
    )
    prev, prev_ghost = cur, ghost_high + ghost_low
    for k in range(DEG):
        ghost = new_ghost if k else ghost_high
        part = elements(cur, ghost, slots, mcat, scales, emat, fmat, qmain, steps)
        cur_ghost = ghost if k else prev_ghost
        new, new_ghost = exchange(coefs[k], part, cur, cur_ghost, prev, prev_ghost, qmain)
        prev, prev_ghost, cur = cur, cur_ghost, new
    filtered, margin = finish(cur, homes.reshape(-1), emat, qmain)
    margin = margin / (states.shape[1] * parts)
    return filtered, margin


def solution(mesh):
    in_specs = (
        P("state", "space"),
        P(),
        P(),
        P(None, "space"),
        P("space"),
        P("space"),
        P("space"),
        P("space"),
    )
    out_specs = (P("state", "space"), P("state", None))
    return jax.shard_map(body, mesh=mesh, in_specs=in_specs, out_specs=out_specs, check_vma=False)
```

```python
import functools

import jax
import jax.numpy as jnp
import numpy as np
from jax import lax
from jax.experimental import pallas as pl
from jax.experimental.pallas import tpu as pltpu
from jax.sharding import PartitionSpec as P

DEG = 4
G = 8
W = 16
LANES = G * W
FACE_LIST = 1024
KU = 5
MESH = pl.DeviceIdType.MESH
F32 = jnp.float32
BF16 = jnp.bfloat16
VMEM_LIMIT = 58 * 2**20


def expand_matrix():
    l = np.arange(LANES)[:, None]
    m = np.arange(G * LANES)[None, :]
    one = (l // W == m // LANES) & (l % W == m % W)
    return jnp.asarray(np.concatenate([one, one], 0), BF16)


def fold_matrix():
    j = np.arange(G)[:, None, None, None]
    l = np.arange(LANES)[None, None, :, None]
    m = np.arange(LANES)[None, None, None, :]
    one = (m // W == j) & (m % W == l % W)
    one = np.broadcast_to(one, (G, 2, LANES, LANES))
    return jnp.asarray(one.reshape(G * 2 * LANES, LANES), BF16)


def split(value):
    high = value.astype(BF16)
    low = (value - high.astype(F32)).astype(BF16)
    return high, low


def lane_group(rows=1):
    return lax.broadcasted_iota(jnp.int32, (rows, LANES), 1) // W


def odd_groups(rows, step):
    return (lane_group(rows) & step) != 0


def merge_groups(rows):
    step = 1
    while len(rows) > 1:
        odd = odd_groups(rows[0].shape[0], step)
        rows = [jnp.where(odd, rows[a + 1], rows[a]) for a in range(0, len(rows), 2)]
        step *= 2
    return rows[0]


def expand_section(src, src_at, dst, dst_at, count, emat, block=512, also=None):
    block = min(block, count)

    def step(i, carry):
        q = pl.multiple_of(i * block, block)
        high, low = split(src[pl.ds(src_at + q, block), :])
        wide = jnp.dot(
            jnp.concatenate([high, low], axis=1), emat[...], preferred_element_type=F32
        )
        for j in range(G):
            dst[pl.ds(dst_at + j * count + q, block), :] = wide[:, j * LANES : (j + 1) * LANES]
        if also is not None:
            also(dst_at + i * block * G, block * G)
        return carry

    lax.fori_loop(0, count // block, step, 0)


def start_lists(source, lists, sems):
    copies = [
        pltpu.make_async_copy(source.at[k], lists[k], sems.at[k]) for k in range(len(lists))
    ]
    for copy in copies:
        copy.start()
    return copies


def start_faces(source, lists, sems):
    size = lists[0].shape[0]
    copies = [
        pltpu.make_async_copy(source.at[pl.ds(k * size, size)], lists[k], sems.at[k])
        for k in range(len(lists))
    ]
    for copy in copies:
        copy.start()
    return copies


def faces_at(lists, count, q):
    inside = lists[0].shape[0] // count
    spots = [q + i * count for i in range(inside)]
    return [lists[j // inside][spots[j % inside]] for j in range(G)]


def states_kernel(
    nmain, nface, core_ref, own, theirs, face_hbm, emat, out, face_high, face_low, X, sems, *faces
):
    qmain, qface = nmain // G, nface // G
    copies = start_faces(face_hbm, faces, sems)
    core = core_ref[0]

    def turn(i, carry):
        q = pl.multiple_of(i * 128, 128)
        parts = []
        for j in range(G):
            a = own[:, pl.ds(j * qmain + q, 128)]
            b = theirs[:, pl.ds(j * qmain + q, 128)]
            parts += [jnp.where(core == 0, a, b), jnp.where(core == 0, b, a)]
        out[pl.ds(q, 128), :] = jnp.concatenate(parts, axis=0).T
        return carry

    lax.fori_loop(0, qmain // 128, turn, 0, unroll=2)
    expand_section(out, 0, X, 0, qmain, emat)
    for copy in copies:
        copy.wait()
    zero = jnp.zeros((1, LANES), F32)

    def take(q, carry):
        nodes = faces_at(faces, qface, q)
        out[pl.ds(qmain + q, 1), :] = merge_groups([X[pl.ds(n, 1), :] for n in nodes])
        for n in nodes:
            X[pl.ds(n, 1), :] = zero
        return carry

    lax.fori_loop(0, qface, take, 0, unroll=8)

    def pack(i, carry):
        q = pl.multiple_of(i * 8, 8)
        out[pl.ds(q, 8), :] = merge_groups([X[pl.ds(j * qmain + q, 8), :] for j in range(G)])
        return carry

    lax.fori_loop(0, qmain // 8, pack, 0, unroll=4)
    face_high[...], face_low[...] = split(out[qmain : qmain + qface, :])


def states_rows(core, own, theirs, face_nodes, emat):
    nmain, nface = own.shape[1], face_nodes.shape[0]
    qmain, qface = nmain // G, nface // G
    vmem = pl.BlockSpec(memory_space=pltpu.VMEM)
    smem = pl.BlockSpec(memory_space=pltpu.SMEM)
    return pl.pallas_call(
        functools.partial(states_kernel, nmain, nface),
        name="states_rows",
        out_shape=[
            jax.ShapeDtypeStruct((qmain + qface, LANES), F32),
            jax.ShapeDtypeStruct((qface, LANES), BF16),
            jax.ShapeDtypeStruct((qface, LANES), BF16),
        ],
        in_specs=[smem, vmem, vmem, pl.BlockSpec(memory_space=pl.ANY), vmem],
        out_specs=[vmem, vmem, vmem],
        scratch_shapes=[
            pltpu.VMEM((nmain, LANES), F32),
            pltpu.SemaphoreType.DMA((nface // FACE_LIST,)),
        ]
        + [pltpu.SMEM((FACE_LIST,), jnp.int32)] * (nface // FACE_LIST),
        compiler_params=pltpu.CompilerParams(vmem_limit_bytes=VMEM_LIMIT),
    )(core, own, theirs, face_nodes, emat)


def prepare_kernel(
    nmain, nface, chunks, after, core_ref, count_ref, bounds, raw, face_rows, matrix, kinetic, potential,
    slots, scales, mcat, *rest
):
    del after
    coefs, padded = rest[:DEG], rest[DEG]
    shape = (8, LANES)
    lowest, lower, upper = (jnp.full(shape, bounds[i], F32) for i in range(3))
    half_width = (upper - lower) / 2.0
    center = (upper + lower) / 2.0
    sigma = half_width / (lowest - center)
    gamma = 2.0 / sigma
    coefs[0][...] = jnp.concatenate([sigma / half_width, jnp.zeros(shape, F32), center], axis=0)
    for k in range(1, DEG):
        following = 1.0 / (gamma - sigma)
        coefs[k][...] = jnp.concatenate(
            [2.0 * following / half_width, sigma * following, center], axis=0
        )
        sigma = following
    core, count = core_ref[0], count_ref[0]
    place = lax.broadcasted_iota(jnp.int32, (1, LANES), 1)
    alive = (core * LANES + place) < count
    lane = lax.broadcasted_iota(jnp.int32, (chunks, LANES), 1)
    chunk = lax.broadcasted_iota(jnp.int32, (chunks, LANES), 0)
    spread = (
        lax.broadcasted_iota(jnp.int32, (LANES, LANES), 0) // chunks
        == lax.broadcasted_iota(jnp.int32, (LANES, LANES), 1) // W
    ).astype(F32)
    for i, (scale, factor) in enumerate(((kinetic, 0.5), (potential, 1.0))):
        row = jnp.where(core == 0, scale[0:1, :], scale[1:2, :]) * factor
        row = jnp.where(alive, row, 0.0)
        wide = jnp.where(lax.rem(lane, chunks) == chunk, row, 0.0)
        scales[i * chunks : (i + 1) * chunks, :] = jnp.dot(
            wide, spread, precision=lax.Precision.HIGHEST, preferred_element_type=F32
        )
    npe = matrix.shape[1]
    padded[...] = jnp.zeros_like(padded)
    padded[0:npe, 0:npe] = matrix[0:npe, :]
    padded[128 : 128 + npe, 0:npe] = matrix[npe : 2 * npe, :]
    high, low = split(padded[...])
    mcat[...] = jnp.concatenate([high, low, high], axis=1)
    hi_count = nmain // 128
    size = 1024
    table = jnp.zeros((256, hi_count), F32)
    for at in range(0, nface, size):
        node = jnp.concatenate(
            [face_rows[r : r + 1, :] for r in range(at // 128, (at + size) // 128)], axis=1
        )
        pos = lax.broadcasted_iota(jnp.int32, (1, size), 1) + (at + 1)
        low = lax.broadcasted_iota(jnp.int32, (128, size), 0) == (node & 127)
        high = lax.broadcasted_iota(jnp.int32, (hi_count, size), 0) == (node >> 7)
        big = jnp.where(low, (pos >> 6).astype(F32), 0.0)
        small = jnp.where(low, (pos & 63).astype(F32), 0.0)
        table += lax.dot_general(
            jnp.concatenate([big, small], axis=0).astype(BF16),
            high.astype(F32).astype(BF16),
            (((1,), (1,)), ((), ())),
            preferred_element_type=F32,
        )
    table = table.astype(BF16)
    width = raw.shape[1]
    owned = (KU - 1) * G
    slots[...] = jnp.zeros_like(slots)
    for k in range(owned):
        node = raw[k : k + 1, :]
        high = lax.broadcasted_iota(jnp.int32, (hi_count, width), 0) == (node >> 7)
        got = jnp.dot(table, high.astype(F32).astype(BF16), preferred_element_type=F32)
        both = got[:128] * 64.0 + got[128:]
        low = lax.broadcasted_iota(jnp.int32, (128, width), 0) == (node & 127)
        pos = jnp.sum(jnp.where(low, both, 0.0), axis=0, keepdims=True).astype(jnp.int32)
        slots[k : k + 1, :width] = jnp.where(pos > 0, nmain + pos - 1, node)
    slots[owned:, :width] = raw[owned:, :] + nface


def prepare(after, core, count, bounds, raw, face_nodes, matrix, kinetic, potential, nmain, chunks):
    nface = face_nodes.shape[0]
    vmem = pl.BlockSpec(memory_space=pltpu.VMEM)
    smem = pl.BlockSpec(memory_space=pltpu.SMEM)
    width = -(-raw.shape[1] // 128) * 128
    return pl.pallas_call(
        functools.partial(prepare_kernel, nmain, nface, chunks),
        name="prepare_lists",
        out_shape=[
            jax.ShapeDtypeStruct((raw.shape[0], width), jnp.int32),
            jax.ShapeDtypeStruct((2 * chunks, LANES), F32),
            jax.ShapeDtypeStruct((256, 384), BF16),
        ]
        + [jax.ShapeDtypeStruct((24, LANES), F32)] * DEG,
        in_specs=[pl.BlockSpec(memory_space=pl.ANY)] + [smem] * 3 + [vmem] * 5,
        out_specs=[vmem] * (3 + DEG),
        scratch_shapes=[pltpu.VMEM((256, 128), F32)],
        compiler_params=pltpu.CompilerParams(vmem_limit_bytes=VMEM_LIMIT),
        cost_estimate=pl.CostEstimate(flops=10**9, bytes_accessed=2**24, transcendentals=0),
    )(
        after, core, count, bounds, raw, face_nodes.reshape(nface // 128, 128), matrix,
        kinetic.reshape(2, LANES), potential.reshape(2, LANES),
    )


def element_kernel(
    sections, chunks, steps, mainface, ghost, slots_hbm, mcat, scales, emat, fmat,
    part, X, acc0, acc1, U, Y, sems, *lists,
):
    copies = start_lists(slots_hbm, lists, sems)
    accs = (acc0, acc1)

    def clear(row, count):
        row = pl.multiple_of(row, count)
        zero = jnp.zeros((count, LANES), F32)
        acc0[pl.ds(row, count), :] = zero
        acc1[pl.ds(row, count), :] = zero

    at = 0
    src, src_at = mainface, 0
    for i, count in enumerate(sections):
        if i == 2:
            src, src_at = ghost, 0
        expand_section(src, src_at, X, at, count, emat, also=clear)
        at += G * count
        src_at += count
    U[:, U.shape[1] - 8 :, :] = jnp.zeros((2, 8, LANES), F32)
    for copy in copies:
        copy.wait()
    group = lane_group()
    masks = [group == j for j in range(G)]

    def gather(c, half, r, b):
        t = (2 * c + half) * steps + r
        rows = [X[pl.ds(lists[b * G + j][t], 1), :] for j in range(G)]
        U[half, pl.ds(b * steps + r, 1), :] = merge_groups(rows)

    def scatter(c, half, r, b):
        t = (2 * c + half) * steps + r
        acc = accs[(b + half) % 2]
        y = Y[half, pl.ds(b * steps + r, 1), :]
        nodes = [lists[b * G + j][t] for j in range(G)]
        sums = [acc[pl.ds(n, 1), :] + y for n in nodes]
        for j in range(G):
            pltpu.store(acc.at[pl.ds(nodes[j], 1), :], sums[j], mask=masks[j])

    def product(c):
        high, low = split(jnp.concatenate([U[0], U[1]], axis=1))
        prod = jnp.dot(
            mcat[...], jnp.concatenate([high, high, low], axis=0), preferred_element_type=F32
        )
        for half in range(2):
            lanes = slice(half * LANES, (half + 1) * LANES)
            kin = scales[pl.ds(2 * c + half, 1), :]
            pot = scales[pl.ds(chunks + 2 * c + half, 1), :]
            Y[half] = kin * prod[:128, lanes] + pot * prod[128:, lanes]

    def loop(*works):
        def step(r, carry):
            for half in range(2):
                for b in range(KU):
                    for work, c in works:
                        work(c, half, r, b)
            return carry

        lax.fori_loop(0, steps, step, 0, unroll=steps)

    loop((gather, 0))

    def chunk(c, carry):
        product(c)
        loop((gather, c + 1), (scatter, c))
        return carry

    pairs = chunks // 2
    lax.fori_loop(0, pairs - 1, chunk, 0)
    product(pairs - 1)
    loop((scatter, pairs - 1))
    at, out_at = 0, 0
    for count in sections:
        block = min(count, 1024)

        def fold(i, carry, at=at, out_at=out_at, count=count, block=block):
            q = pl.multiple_of(i * block, block)
            pieces = []
            for j in range(G):
                rows = pl.ds(at + j * count + q, block)
                pieces.extend(split(acc0[rows, :] + acc1[rows, :]))
            part[pl.ds(out_at + q, block), :] = jnp.dot(
                jnp.concatenate(pieces, axis=1), fmat[...], preferred_element_type=F32
            )
            return carry

        lax.fori_loop(0, count // block, fold, 0)
        at += G * count
        out_at += count


def elements(mainface, ghost, slots, mcat, scales, emat, fmat, qmain, steps):
    qface = mainface.shape[0] - qmain
    sections = (qmain, qface, ghost.shape[0])
    total = sum(sections)
    chunks = scales.shape[0] // 2
    vmem = pl.BlockSpec(memory_space=pltpu.VMEM)
    return pl.pallas_call(
        functools.partial(element_kernel, sections, chunks, steps),
        name="element_rows",
        out_shape=jax.ShapeDtypeStruct((total, LANES), F32),
        in_specs=[vmem, vmem, pl.BlockSpec(memory_space=pl.ANY)] + [vmem] * 4,
        out_specs=vmem,
        scratch_shapes=[pltpu.VMEM((G * total, LANES), F32)] * 3
        + [pltpu.VMEM((2, 128, LANES), F32)] * 2
        + [pltpu.SemaphoreType.DMA((KU * G,))]
        + [pltpu.SMEM((slots.shape[1],), jnp.int32)] * (KU * G),
        compiler_params=pltpu.CompilerParams(vmem_limit_bytes=VMEM_LIMIT),
    )(mainface, ghost, slots, mcat, scales, emat, fmat)


def exchange_kernel(
    qmain, qface, parts, coef, part, cur_in, cur_ghost_in, prev_in, prev_ghost_in, out, out_ghost,
    own, cur, cur_ghost, prev, prev_ghost, theirs, new, new_ghost, up_send, down_send, from_below, from_above,
    load_sem, store_sem, send_sem, recv_sem, side_send, side_recv, relay_send, relay_recv,
):
    pieces = 4
    rows = qmain // pieces
    half = qface // 2
    space, state = lax.axis_index("space"), lax.axis_index("state")
    core = lax.rem(state, 2)
    other = state + 1 - 2 * core
    above = lax.rem(space + 1, parts)
    below = lax.rem(space + parts - 1, parts)
    loads = []
    for src, dst in (
        (part, own), (cur_in, cur), (prev_in, prev), (cur_ghost_in, cur_ghost), (prev_ghost_in, prev_ghost)
    ):
        load = pltpu.make_async_copy(src, dst, load_sem.at[len(loads)])
        load.start()
        loads.append(load)
    barrier = pltpu.get_barrier_semaphore()
    for device in ((space, other), (above, state), (below, state)):
        pl.semaphore_signal(barrier, inc=1, device_id=device, device_id_type=MESH)
    pl.semaphore_wait(barrier, 3)

    mine = pl.multiple_of(core * half, half)
    not_mine = pl.multiple_of((1 - core) * half, half)
    face_at, ghost_at = qmain, qmain + qface
    spans = (
        [pl.ds(face_at + not_mine, half), pl.ds(ghost_at + not_mine, half)]
        + [pl.ds(i * rows, rows) for i in range(pieces)]
        + [pl.ds(face_at + mine, half), pl.ds(ghost_at + mine, half)]
    )
    swaps = []
    for i, span in enumerate(spans):
        swap = pltpu.make_async_remote_copy(
            src_ref=part.at[span, :], dst_ref=theirs.at[span, :],
            send_sem=send_sem.at[i], recv_sem=recv_sem.at[i],
            device_id=(space, other), device_id_type=MESH,
        )
        swap.start()
        swaps.append(swap)

    def arrived(i, span):
        pltpu.make_async_remote_copy(
            src_ref=part.at[span, :], dst_ref=theirs.at[span, :],
            send_sem=send_sem.at[i], recv_sem=recv_sem.at[i],
            device_id=(space, other), device_id_type=MESH,
        ).wait_recv()

    loads[0].wait()
    face_mine, ghost_mine = pl.ds(face_at + mine, half), pl.ds(ghost_at + mine, half)
    face_other, ghost_other = pl.ds(face_at + not_mine, half), pl.ds(ghost_at + not_mine, half)
    here, there = pl.ds(mine, half), pl.ds(not_mine, half)
    arrived(0, face_mine)
    down_send[...] = (own[face_mine, :] + theirs[face_mine, :]).astype(BF16)
    arrived(1, ghost_mine)
    up_send[...] = (own[ghost_mine, :] + theirs[ghost_mine, :]).astype(BF16)
    sides = []
    for i, (src, dst, place) in enumerate(
        ((up_send, from_below, above), (down_send, from_above, below))
    ):
        side = pltpu.make_async_remote_copy(
            src_ref=src, dst_ref=dst.at[here, :],
            send_sem=side_send.at[i], recv_sem=side_recv.at[i],
            device_id=(place, state), device_id_type=MESH,
        )
        side.start()
        sides.append(side)

    for load in loads[1:]:
        load.wait()
    gain, damp, center = coef[0:1, :], coef[8:9, :], coef[16:17, :]

    def step(h, now, before):
        return (h - center * now) * gain - damp * before

    stores = []

    def keep(src, dst, span):
        copy = pltpu.make_async_copy(
            src.at[span, :], dst.at[span, :], store_sem.at[len(stores)]
        )
        copy.start()
        stores.append(copy)

    for i in range(pieces):
        span = spans[i + 2]
        swaps[i + 2].wait_recv()
        new[span, :] = step(own[span, :] + theirs[span, :], cur[span, :], prev[span, :])
        keep(new, out, span)
    arrived(6, face_other)
    arrived(7, ghost_other)
    relays = []
    for i, dst in enumerate((from_below, from_above)):
        sides[i].wait_recv()
        relay = pltpu.make_async_remote_copy(
            src_ref=dst.at[here, :], dst_ref=dst.at[here, :],
            send_sem=relay_send.at[i], recv_sem=relay_recv.at[i],
            device_id=(space, other), device_id_type=MESH,
        )
        relay.start()
        relays.append(relay)

    def finish(face_span, ghost_span, span):
        h = own[face_span, :] + theirs[face_span, :]
        extra = from_below[span, :].astype(F32)
        h = h + jnp.where(space == 0, jnp.zeros_like(extra), extra)
        new[face_span, :] = step(h, cur[face_span, :], prev[face_span, :])
        keep(new, out, face_span)
        h = own[ghost_span, :] + theirs[ghost_span, :] + from_above[span, :].astype(F32)
        h = jnp.where(space == parts - 1, jnp.zeros_like(h), h)
        new_ghost[span, :] = step(h, cur_ghost[span, :], prev_ghost[span, :])
        keep(new_ghost, out_ghost, span)

    finish(face_mine, ghost_mine, here)
    for i, dst in enumerate((from_below, from_above)):
        pltpu.make_async_remote_copy(
            src_ref=dst.at[there, :], dst_ref=dst.at[there, :],
            send_sem=relay_send.at[i], recv_sem=relay_recv.at[i],
            device_id=(space, other), device_id_type=MESH,
        ).wait_recv()
    finish(face_other, ghost_other, there)
    for copy in swaps + sides + relays:
        copy.wait_send()
    for copy in stores:
        copy.wait()


def exchange(coef, part, cur, cur_ghost, prev, prev_ghost, qmain):
    qface = cur_ghost.shape[0]
    parts = lax.axis_size("space")
    hbm = pl.BlockSpec(memory_space=pltpu.HBM)
    half = qface // 2
    return pl.pallas_call(
        functools.partial(exchange_kernel, qmain, qface, parts),
        name="exchange_update",
        out_shape=[
            jax.ShapeDtypeStruct(cur.shape, F32),
            jax.ShapeDtypeStruct(cur_ghost.shape, F32),
        ],
        in_specs=[pl.BlockSpec(memory_space=pltpu.VMEM)] + [hbm] * 5,
        out_specs=[hbm, hbm],
        scratch_shapes=[
            pltpu.VMEM(part.shape, F32),
            pltpu.VMEM(cur.shape, F32),
            pltpu.VMEM(cur_ghost.shape, F32),
            pltpu.VMEM(cur.shape, F32),
            pltpu.VMEM(cur_ghost.shape, F32),
            pltpu.VMEM(part.shape, F32),
            pltpu.VMEM(cur.shape, F32),
            pltpu.VMEM(cur_ghost.shape, F32),
            pltpu.VMEM((half, LANES), BF16),
            pltpu.VMEM((half, LANES), BF16),
            pltpu.VMEM((qface, LANES), BF16),
            pltpu.VMEM((qface, LANES), BF16),
            pltpu.SemaphoreType.DMA((5,)),
            pltpu.SemaphoreType.DMA((8,)),
            pltpu.SemaphoreType.DMA((8,)),
            pltpu.SemaphoreType.DMA((8,)),
            pltpu.SemaphoreType.DMA((2,)),
            pltpu.SemaphoreType.DMA((2,)),
            pltpu.SemaphoreType.DMA((2,)),
            pltpu.SemaphoreType.DMA((2,)),
        ],
        compiler_params=pltpu.CompilerParams(
            collective_id=0, has_side_effects=True, vmem_limit_bytes=VMEM_LIMIT
        ),
    )(coef, part, cur, cur_ghost, prev, prev_ghost)


def margin_kernel(grid, rounded, out, blocks, gram, sums, across, along, *sems):
    depth, width, ring = grid
    space, state = lax.axis_index("space"), lax.axis_index("state")
    z, x = space // width, lax.rem(space, width)
    y, core = state // 2, lax.rem(state, 2)
    chips = ring // 2
    state_send, state_recv, row_send, row_recv, x_send, x_recv, z_send, z_recv = sems
    friends = [(space, lax.rem(state + k, ring)) for k in range(1, ring)]
    x_friends = [(z * width + lax.rem(x + k, width), state) for k in range(1, width)]
    z_friends = [(lax.rem(z + k, depth) * width + x, state) for k in range(1, depth)]
    barrier = pltpu.get_barrier_semaphore()
    everyone = friends + x_friends + z_friends
    for device in everyone:
        pl.semaphore_signal(barrier, inc=1, device_id=device, device_id_type=MESH)
    pl.semaphore_wait(barrier, len(everyone))

    copies = []
    for k in range(1, chips):
        to = lax.rem(y + k, chips)
        copy = pltpu.make_async_remote_copy(
            src_ref=rounded.at[to], dst_ref=blocks.at[k],
            send_sem=state_send.at[k], recv_sem=state_recv.at[k],
            device_id=(space, 2 * to + core), device_id_type=MESH,
        )
        copy.start()
        copies.append(copy)
    blocks[0] = rounded[y]
    for copy in copies:
        copy.wait()
    ordered = jnp.concatenate([blocks[lax.rem(y + chips - i, chips)] for i in range(chips)], axis=0)
    gram[:, : ordered.shape[0]] = lax.dot_general(
        ordered, ordered, (((1,), (1,)), ((), ())), preferred_element_type=F32
    )
    gram[:, ordered.shape[0] :] = jnp.zeros_like(gram[:, ordered.shape[0] :])

    def add_up(sources, friends, slots, send, recv):
        copies = []
        for k, (src, device) in enumerate(zip(sources, friends), 1):
            copy = pltpu.make_async_remote_copy(
                src_ref=src, dst_ref=slots.at[k], send_sem=send.at[k], recv_sem=recv.at[k],
                device_id=device, device_id_type=MESH,
            )
            copy.start()
            copies.append(copy)
        for copy in copies:
            copy.wait()
        return functools.reduce(lambda a, b: a + b, [slots[k] for k in range(1, len(friends) + 1)])

    def rows_of(member):
        return pl.ds(pl.multiple_of(member * 8, 8), 8)

    rows = [gram.at[rows_of(device[1]), :] for device in friends]
    total = gram[rows_of(state), :] + add_up(rows, friends, sums, row_send, row_recv)
    across[0] = total
    total = total + add_up([across.at[0]] * (width - 1), x_friends, across, x_send, x_recv)
    along[0] = total
    total = total + add_up([along.at[0]] * (depth - 1), z_friends, along, z_send, z_recv)
    out[...] = total[:, : out.shape[1]]


def margin_of(rounded):
    ring = lax.axis_size("state")
    parts = lax.axis_size("space")
    width = 4
    depth = parts // width
    chips = ring // 2
    count = 8 * ring
    vmem = pl.BlockSpec(memory_space=pltpu.VMEM)
    sems = [pltpu.SemaphoreType.DMA((n,)) for n in (chips, chips, ring, ring, width, width, depth, depth)]
    return pl.pallas_call(
        functools.partial(margin_kernel, (depth, width, ring)),
        name="margin_rows",
        out_shape=jax.ShapeDtypeStruct((8, count), F32),
        in_specs=[vmem],
        out_specs=vmem,
        scratch_shapes=[
            pltpu.VMEM(rounded.shape, BF16),
            pltpu.VMEM((count, LANES), F32),
            pltpu.VMEM((ring, 8, LANES), F32),
            pltpu.VMEM((width, 8, LANES), F32),
            pltpu.VMEM((depth, 8, LANES), F32),
        ]
        + sems,
        compiler_params=pltpu.CompilerParams(
            collective_id=1, has_side_effects=True, vmem_limit_bytes=VMEM_LIMIT
        ),
    )(rounded)


def final_kernel(qmain, qface, core_ref, mainface, face_hbm, emat, out, rounded, X, R, sems, *faces):
    copies = start_faces(face_hbm, faces, sems)
    expand_section(mainface, 0, X, 0, qmain, emat)
    expand_section(mainface, qmain, R, 0, qface, emat)
    for copy in copies:
        copy.wait()

    def put(q, carry):
        for j, n in enumerate(faces_at(faces, qface, q)):
            X[pl.ds(n, 1), :] = R[pl.ds(j * qface + q, 1), :]
        return carry

    lax.fori_loop(0, qface, put, 0, unroll=4)
    core = core_ref[0]

    def turn(i, carry):
        q = pl.multiple_of(i * 128, 128)
        rows = merge_groups([X[pl.ds(j * qmain + q, 128), :] for j in range(G)]).T
        for j in range(G):
            a = rows[j * W : j * W + 8]
            b = rows[j * W + 8 : j * W + 16]
            out[:, pl.ds(j * qmain + q, 128)] = jnp.where(core == 0, a, b)
        far = G // 2
        for j in range(far):
            a = rows[j * W : (j + 1) * W]
            b = rows[(far + j) * W : (far + j + 1) * W]
            rounded[j, :, pl.ds(q, 128)] = jnp.where(core == 0, a, b).astype(BF16)
        return carry

    lax.fori_loop(0, qmain // 128, turn, 0)


def final(core, mainface, face_nodes, emat, qmain):
    qface = mainface.shape[0] - qmain
    vmem = pl.BlockSpec(memory_space=pltpu.VMEM)
    return pl.pallas_call(
        functools.partial(final_kernel, qmain, qface),
        name="final_block",
        out_shape=[
            jax.ShapeDtypeStruct((8, G * qmain), F32),
            jax.ShapeDtypeStruct((G // 2, W, qmain), BF16),
        ],
        in_specs=[
            pl.BlockSpec(memory_space=pltpu.SMEM), vmem, pl.BlockSpec(memory_space=pl.ANY), vmem
        ],
        out_specs=[vmem, vmem],
        scratch_shapes=[
            pltpu.VMEM((G * qmain, LANES), F32),
            pltpu.VMEM((G * qface, LANES), F32),
            pltpu.SemaphoreType.DMA((G * qface // FACE_LIST,)),
        ]
        + [pltpu.SMEM((FACE_LIST,), jnp.int32)] * (G * qface // FACE_LIST),
        compiler_params=pltpu.CompilerParams(vmem_limit_bytes=VMEM_LIMIT),
    )(core, mainface, face_nodes, emat)


def body(states, bounds, element_matrix, elem_nodes, face_nodes, kinetic, potential, elem_count):
    parts = lax.axis_size("space")
    members = lax.axis_size("state")
    core = lax.rem(lax.axis_index("state"), 2)
    npe, slot_count = elem_nodes.shape
    half = slot_count // 2
    chunks = half // G
    steps = npe // KU
    qmain = states.shape[1] // G

    mine = lax.dynamic_slice(elem_nodes, (0, core * half), (npe, half))
    raw = mine.reshape(KU, steps, G, chunks).transpose(0, 2, 3, 1).reshape(KU * G, chunks * steps)
    emat, fmat = expand_matrix(), fold_matrix()
    which = core.reshape(1)

    partner = lax.ppermute(states, "state", [(i, i ^ 1) for i in range(members)])
    cur, face_high, face_low = states_rows(which, states, partner, face_nodes, emat)
    downwards = [(i, i - 1) for i in range(1, parts)]
    ghost_high = lax.ppermute(face_high, "space", downwards).astype(F32)
    ghost_low = lax.ppermute(face_low, "space", downwards).astype(F32)
    slots, scales, mcat, *coefs = prepare(
        face_low, which, elem_count, bounds, raw, face_nodes, element_matrix, kinetic, potential,
        states.shape[1], chunks,
    )
    prev, prev_ghost = cur, ghost_high + ghost_low
    for k in range(DEG):
        ghost = new_ghost if k else ghost_high
        part = elements(cur, ghost, slots, mcat, scales, emat, fmat, qmain, steps)
        cur_ghost = ghost if k else prev_ghost
        new, new_ghost = exchange(coefs[k], part, cur, cur_ghost, prev, prev_ghost, qmain)
        prev, prev_ghost, cur = cur, cur_ghost, new
    filtered, rounded = final(which, cur, face_nodes, emat, qmain)
    margin = margin_of(rounded) / (states.shape[1] * parts)
    return filtered, margin


def solution(mesh):
    in_specs = (
        P("state", "space"),
        P(),
        P(),
        P(None, "space"),
        P("space"),
        P("space"),
        P("space"),
        P("space"),
    )
    out_specs = (P("state", "space"), P("state", None))
    return jax.shard_map(body, mesh=mesh, in_specs=in_specs, out_specs=out_specs, check_vma=False)
```

```python
import functools

import jax
import jax.numpy as jnp
import numpy as np
from jax import lax
from jax.experimental import pallas as pl
from jax.experimental.pallas import tpu as pltpu
from jax.sharding import PartitionSpec as P

DEG = 4
G = 8
W = 16
LANES = G * W
FACE_LIST = 1024
KU = 5
MESH = pl.DeviceIdType.MESH
F32 = jnp.float32
BF16 = jnp.bfloat16
VMEM_LIMIT = 58 * 2**20


def expand_matrix():
    l = np.arange(LANES)[:, None]
    m = np.arange(G * LANES)[None, :]
    one = (l // W == m // LANES) & (l % W == m % W)
    return jnp.asarray(np.concatenate([one, one], 0), BF16)


def fold_matrix():
    j = np.arange(G)[:, None, None, None]
    l = np.arange(LANES)[None, None, :, None]
    m = np.arange(LANES)[None, None, None, :]
    one = (m // W == j) & (m % W == l % W)
    one = np.broadcast_to(one, (G, 2, LANES, LANES))
    return jnp.asarray(one.reshape(G * 2 * LANES, LANES), BF16)


def split(value):
    high = value.astype(BF16)
    low = (value - high.astype(F32)).astype(BF16)
    return high, low


def lane_group(rows=1):
    return lax.broadcasted_iota(jnp.int32, (rows, LANES), 1) // W


def odd_groups(rows, step):
    return (lane_group(rows) & step) != 0


def merge_groups(rows):
    step = 1
    while len(rows) > 1:
        odd = odd_groups(rows[0].shape[0], step)
        rows = [jnp.where(odd, rows[a + 1], rows[a]) for a in range(0, len(rows), 2)]
        step *= 2
    return rows[0]


def expand_section(src, src_at, dst, dst_at, count, emat, block=512, also=None):
    block = min(block, count)

    def step(i, carry):
        q = pl.multiple_of(i * block, block)
        high, low = split(src[pl.ds(src_at + q, block), :])
        wide = jnp.dot(
            jnp.concatenate([high, low], axis=1), emat[...], preferred_element_type=F32
        )
        for j in range(G):
            dst[pl.ds(dst_at + j * count + q, block), :] = wide[:, j * LANES : (j + 1) * LANES]
        if also is not None:
            also(dst_at + i * block * G, block * G)
        return carry

    lax.fori_loop(0, count // block, step, 0)


def start_lists(source, lists, sems):
    copies = [
        pltpu.make_async_copy(source.at[k], lists[k], sems.at[k]) for k in range(len(lists))
    ]
    for copy in copies:
        copy.start()
    return copies


def start_faces(source, lists, sems):
    size = lists[0].shape[0]
    copies = [
        pltpu.make_async_copy(source.at[pl.ds(k * size, size)], lists[k], sems.at[k])
        for k in range(len(lists))
    ]
    for copy in copies:
        copy.start()
    return copies


def faces_at(lists, count, q):
    inside = lists[0].shape[0] // count
    spots = [q + i * count for i in range(inside)]
    return [lists[j // inside][spots[j % inside]] for j in range(G)]


def states_kernel(
    nmain, nface, core_ref, own, theirs, face_hbm, emat, out, face_high, face_low, X, sems, *faces
):
    qmain, qface = nmain // G, nface // G
    copies = start_faces(face_hbm, faces, sems)
    core = core_ref[0]

    def turn(i, carry):
        q = pl.multiple_of(i * 128, 128)
        parts = []
        for j in range(G):
            a = own[:, pl.ds(j * qmain + q, 128)]
            b = theirs[:, pl.ds(j * qmain + q, 128)]
            parts += [jnp.where(core == 0, a, b), jnp.where(core == 0, b, a)]
        out[pl.ds(q, 128), :] = jnp.concatenate(parts, axis=0).T
        return carry

    lax.fori_loop(0, qmain // 128, turn, 0, unroll=2)
    expand_section(out, 0, X, 0, qmain, emat)
    for copy in copies:
        copy.wait()
    zero = jnp.zeros((1, LANES), F32)

    def take(q, carry):
        nodes = faces_at(faces, qface, q)
        out[pl.ds(qmain + q, 1), :] = merge_groups([X[pl.ds(n, 1), :] for n in nodes])
        for n in nodes:
            X[pl.ds(n, 1), :] = zero
        return carry

    lax.fori_loop(0, qface, take, 0, unroll=8)

    def pack(i, carry):
        q = pl.multiple_of(i * 8, 8)
        out[pl.ds(q, 8), :] = merge_groups([X[pl.ds(j * qmain + q, 8), :] for j in range(G)])
        return carry

    lax.fori_loop(0, qmain // 8, pack, 0, unroll=4)
    face_high[...], face_low[...] = split(out[qmain : qmain + qface, :])


def states_rows(core, own, theirs, face_nodes, emat):
    nmain, nface = own.shape[1], face_nodes.shape[0]
    qmain, qface = nmain // G, nface // G
    vmem = pl.BlockSpec(memory_space=pltpu.VMEM)
    smem = pl.BlockSpec(memory_space=pltpu.SMEM)
    return pl.pallas_call(
        functools.partial(states_kernel, nmain, nface),
        name="states_rows",
        out_shape=[
            jax.ShapeDtypeStruct((qmain + qface, LANES), F32),
            jax.ShapeDtypeStruct((qface, LANES), BF16),
            jax.ShapeDtypeStruct((qface, LANES), BF16),
        ],
        in_specs=[smem, vmem, vmem, pl.BlockSpec(memory_space=pl.ANY), vmem],
        out_specs=[vmem, vmem, vmem],
        scratch_shapes=[
            pltpu.VMEM((nmain, LANES), F32),
            pltpu.SemaphoreType.DMA((nface // FACE_LIST,)),
        ]
        + [pltpu.SMEM((FACE_LIST,), jnp.int32)] * (nface // FACE_LIST),
        compiler_params=pltpu.CompilerParams(vmem_limit_bytes=VMEM_LIMIT),
    )(core, own, theirs, face_nodes, emat)


def prepare_kernel(
    nmain, nface, chunks, after, core_ref, count_ref, bounds, raw, face_rows, matrix, kinetic, potential,
    slots, scales, mcat, *rest
):
    del after
    coefs, padded = rest[:DEG], rest[DEG]
    shape = (8, LANES)
    lowest, lower, upper = (jnp.full(shape, bounds[i], F32) for i in range(3))
    half_width = (upper - lower) / 2.0
    center = (upper + lower) / 2.0
    sigma = half_width / (lowest - center)
    gamma = 2.0 / sigma
    coefs[0][...] = jnp.concatenate([sigma / half_width, jnp.zeros(shape, F32), center], axis=0)
    for k in range(1, DEG):
        following = 1.0 / (gamma - sigma)
        coefs[k][...] = jnp.concatenate(
            [2.0 * following / half_width, sigma * following, center], axis=0
        )
        sigma = following
    core, count = core_ref[0], count_ref[0]
    place = lax.broadcasted_iota(jnp.int32, (1, LANES), 1)
    alive = (core * LANES + place) < count
    lane = lax.broadcasted_iota(jnp.int32, (chunks, LANES), 1)
    chunk = lax.broadcasted_iota(jnp.int32, (chunks, LANES), 0)
    spread = (
        lax.broadcasted_iota(jnp.int32, (LANES, LANES), 0) // chunks
        == lax.broadcasted_iota(jnp.int32, (LANES, LANES), 1) // W
    ).astype(F32)
    for i, (scale, factor) in enumerate(((kinetic, 0.5), (potential, 1.0))):
        row = jnp.where(core == 0, scale[0:1, :], scale[1:2, :]) * factor
        row = jnp.where(alive, row, 0.0)
        wide = jnp.where(lax.rem(lane, chunks) == chunk, row, 0.0)
        scales[i * chunks : (i + 1) * chunks, :] = jnp.dot(
            wide, spread, precision=lax.Precision.HIGHEST, preferred_element_type=F32
        )
    npe = matrix.shape[1]
    padded[...] = jnp.zeros_like(padded)
    padded[0:npe, 0:npe] = matrix[0:npe, :]
    padded[128 : 128 + npe, 0:npe] = matrix[npe : 2 * npe, :]
    high, low = split(padded[...])
    mcat[...] = jnp.concatenate([high, low, high], axis=1)
    hi_count = nmain // 128
    size = 1024
    table = jnp.zeros((256, hi_count), F32)
    for at in range(0, nface, size):
        node = jnp.concatenate(
            [face_rows[r : r + 1, :] for r in range(at // 128, (at + size) // 128)], axis=1
        )
        pos = lax.broadcasted_iota(jnp.int32, (1, size), 1) + (at + 1)
        low = lax.broadcasted_iota(jnp.int32, (128, size), 0) == (node & 127)
        high = lax.broadcasted_iota(jnp.int32, (hi_count, size), 0) == (node >> 7)
        big = jnp.where(low, (pos >> 6).astype(F32), 0.0)
        small = jnp.where(low, (pos & 63).astype(F32), 0.0)
        table += lax.dot_general(
            jnp.concatenate([big, small], axis=0).astype(BF16),
            high.astype(F32).astype(BF16),
            (((1,), (1,)), ((), ())),
            preferred_element_type=F32,
        )
    table = table.astype(BF16)
    width = raw.shape[1]
    owned = (KU - 1) * G
    slots[...] = jnp.zeros_like(slots)
    for k in range(owned):
        node = raw[k : k + 1, :]
        high = lax.broadcasted_iota(jnp.int32, (hi_count, width), 0) == (node >> 7)
        got = jnp.dot(table, high.astype(F32).astype(BF16), preferred_element_type=F32)
        both = got[:128] * 64.0 + got[128:]
        low = lax.broadcasted_iota(jnp.int32, (128, width), 0) == (node & 127)
        pos = jnp.sum(jnp.where(low, both, 0.0), axis=0, keepdims=True).astype(jnp.int32)
        slots[k : k + 1, :width] = jnp.where(pos > 0, nmain + pos - 1, node)
    slots[owned:, :width] = raw[owned:, :] + nface


def prepare(after, core, count, bounds, raw, face_nodes, matrix, kinetic, potential, nmain, chunks):
    nface = face_nodes.shape[0]
    vmem = pl.BlockSpec(memory_space=pltpu.VMEM)
    smem = pl.BlockSpec(memory_space=pltpu.SMEM)
    width = -(-raw.shape[1] // 128) * 128
    return pl.pallas_call(
        functools.partial(prepare_kernel, nmain, nface, chunks),
        name="prepare_lists",
        out_shape=[
            jax.ShapeDtypeStruct((raw.shape[0], width), jnp.int32),
            jax.ShapeDtypeStruct((2 * chunks, LANES), F32),
            jax.ShapeDtypeStruct((256, 384), BF16),
        ]
        + [jax.ShapeDtypeStruct((24, LANES), F32)] * DEG,
        in_specs=[pl.BlockSpec(memory_space=pl.ANY)] + [smem] * 3 + [vmem] * 5,
        out_specs=[vmem] * (3 + DEG),
        scratch_shapes=[pltpu.VMEM((256, 128), F32)],
        compiler_params=pltpu.CompilerParams(vmem_limit_bytes=VMEM_LIMIT),
        cost_estimate=pl.CostEstimate(flops=10**9, bytes_accessed=2**24, transcendentals=0),
    )(
        after, core, count, bounds, raw, face_nodes.reshape(nface // 128, 128), matrix,
        kinetic.reshape(2, LANES), potential.reshape(2, LANES),
    )


def element_kernel(
    sections, chunks, steps, mainface, ghost, slots_hbm, mcat, scales, emat, fmat,
    out, X, acc0, acc1, U, Y, part, sems, out_sems, *lists,
):
    copies = start_lists(slots_hbm, lists, sems)
    accs = (acc0, acc1)

    def clear(row, count):
        row = pl.multiple_of(row, count)
        zero = jnp.zeros((count, LANES), F32)
        acc0[pl.ds(row, count), :] = zero
        acc1[pl.ds(row, count), :] = zero

    at = 0
    src, src_at = mainface, 0
    for i, count in enumerate(sections):
        if i == 2:
            src, src_at = ghost, 0
        expand_section(src, src_at, X, at, count, emat, also=clear)
        at += G * count
        src_at += count
    U[:, U.shape[1] - 8 :, :] = jnp.zeros((2, 8, LANES), F32)
    for copy in copies:
        copy.wait()
    group = lane_group()
    masks = [group == j for j in range(G)]

    def gather(c, half, r, b):
        t = (2 * c + half) * steps + r
        rows = [X[pl.ds(lists[b * G + j][t], 1), :] for j in range(G)]
        U[half, pl.ds(b * steps + r, 1), :] = merge_groups(rows)

    def scatter(c, half, r, b):
        t = (2 * c + half) * steps + r
        acc = accs[(b + half) % 2]
        y = Y[half, pl.ds(b * steps + r, 1), :]
        nodes = [lists[b * G + j][t] for j in range(G)]
        sums = [acc[pl.ds(n, 1), :] + y for n in nodes]
        for j in range(G):
            pltpu.store(acc.at[pl.ds(nodes[j], 1), :], sums[j], mask=masks[j])

    def product(c):
        high, low = split(jnp.concatenate([U[0], U[1]], axis=1))
        prod = jnp.dot(
            mcat[...], jnp.concatenate([high, high, low], axis=0), preferred_element_type=F32
        )
        for half in range(2):
            lanes = slice(half * LANES, (half + 1) * LANES)
            kin = scales[pl.ds(2 * c + half, 1), :]
            pot = scales[pl.ds(chunks + 2 * c + half, 1), :]
            Y[half] = kin * prod[:128, lanes] + pot * prod[128:, lanes]

    def loop(*works):
        def step(r, carry):
            for half in range(2):
                for b in range(KU):
                    for work, c in works:
                        work(c, half, r, b)
            return carry

        lax.fori_loop(0, steps, step, 0, unroll=steps)

    loop((gather, 0))

    def chunk(c, carry):
        product(c)
        loop((gather, c + 1), (scatter, c))
        return carry

    pairs = chunks // 2
    lax.fori_loop(0, pairs - 1, chunk, 0)
    product(pairs - 1)
    loop((scatter, pairs - 1))
    at, out_at = 0, 0
    stores = []
    for count in sections:
        block = min(count, 1024)

        def store(i, out_at=out_at, block=block, first=len(stores)):
            rows = pl.ds(pl.multiple_of(out_at + i * block, 8), block)
            return pltpu.make_async_copy(part.at[rows, :], out.at[rows, :], out_sems.at[first + i])

        def fold(i, carry, at=at, out_at=out_at, count=count, block=block, store=store):
            q = pl.multiple_of(i * block, block)
            pieces = []
            for j in range(G):
                rows = pl.ds(at + j * count + q, block)
                pieces.extend(split(acc0[rows, :] + acc1[rows, :]))
            part[pl.ds(out_at + q, block), :] = jnp.dot(
                jnp.concatenate(pieces, axis=1), fmat[...], preferred_element_type=F32
            )
            store(i).start()
            return carry

        lax.fori_loop(0, count // block, fold, 0)
        stores += [store(i) for i in range(count // block)]
        at += G * count
        out_at += count
    for copy in stores:
        copy.wait()


def elements(mainface, ghost, slots, mcat, scales, emat, fmat, qmain, steps):
    qface = mainface.shape[0] - qmain
    sections = (qmain, qface, ghost.shape[0])
    total = sum(sections)
    chunks = scales.shape[0] // 2
    vmem = pl.BlockSpec(memory_space=pltpu.VMEM)
    return pl.pallas_call(
        functools.partial(element_kernel, sections, chunks, steps),
        name="element_rows",
        out_shape=jax.ShapeDtypeStruct((total, LANES), F32),
        in_specs=[vmem, vmem, pl.BlockSpec(memory_space=pl.ANY)] + [vmem] * 4,
        out_specs=pl.BlockSpec(memory_space=pl.ANY),
        scratch_shapes=[pltpu.VMEM((G * total, LANES), F32)] * 3
        + [pltpu.VMEM((2, 128, LANES), F32)] * 2
        + [pltpu.VMEM((total, LANES), F32)]
        + [pltpu.SemaphoreType.DMA((KU * G,)), pltpu.SemaphoreType.DMA((4,))]
        + [pltpu.SMEM((slots.shape[1],), jnp.int32)] * (KU * G),
        compiler_params=pltpu.CompilerParams(vmem_limit_bytes=VMEM_LIMIT),
    )(mainface, ghost, slots, mcat, scales, emat, fmat)


def exchange_kernel(
    qmain, qface, parts, coef, part, cur_in, cur_ghost_in, prev_in, prev_ghost_in, out, out_ghost,
    own, cur, cur_ghost, prev, prev_ghost, theirs, new, new_ghost, up_send, down_send, from_below, from_above,
    load_sem, store_sem, send_sem, recv_sem, side_send, side_recv, relay_send, relay_recv,
):
    pieces = 4
    rows = qmain // pieces
    half = qface // 2
    space, state = lax.axis_index("space"), lax.axis_index("state")
    core = lax.rem(state, 2)
    other = state + 1 - 2 * core
    above = lax.rem(space + 1, parts)
    below = lax.rem(space + parts - 1, parts)
    loads = []
    for src, dst in (
        (part, own), (cur_in, cur), (prev_in, prev), (cur_ghost_in, cur_ghost), (prev_ghost_in, prev_ghost)
    ):
        load = pltpu.make_async_copy(src, dst, load_sem.at[len(loads)])
        load.start()
        loads.append(load)
    barrier = pltpu.get_barrier_semaphore()
    for device in ((space, other), (above, state), (below, state)):
        pl.semaphore_signal(barrier, inc=1, device_id=device, device_id_type=MESH)
    pl.semaphore_wait(barrier, 3)

    mine = pl.multiple_of(core * half, half)
    not_mine = pl.multiple_of((1 - core) * half, half)
    face_at, ghost_at = qmain, qmain + qface
    spans = (
        [pl.ds(face_at + not_mine, half), pl.ds(ghost_at + not_mine, half)]
        + [pl.ds(i * rows, rows) for i in range(pieces)]
        + [pl.ds(face_at + mine, half), pl.ds(ghost_at + mine, half)]
    )
    swaps = []
    for i, span in enumerate(spans):
        swap = pltpu.make_async_remote_copy(
            src_ref=part.at[span, :], dst_ref=theirs.at[span, :],
            send_sem=send_sem.at[i], recv_sem=recv_sem.at[i],
            device_id=(space, other), device_id_type=MESH,
        )
        swap.start()
        swaps.append(swap)

    def arrived(i, span):
        pltpu.make_async_remote_copy(
            src_ref=part.at[span, :], dst_ref=theirs.at[span, :],
            send_sem=send_sem.at[i], recv_sem=recv_sem.at[i],
            device_id=(space, other), device_id_type=MESH,
        ).wait_recv()

    loads[0].wait()
    face_mine, ghost_mine = pl.ds(face_at + mine, half), pl.ds(ghost_at + mine, half)
    face_other, ghost_other = pl.ds(face_at + not_mine, half), pl.ds(ghost_at + not_mine, half)
    here, there = pl.ds(mine, half), pl.ds(not_mine, half)
    arrived(0, face_mine)
    down_send[...] = (own[face_mine, :] + theirs[face_mine, :]).astype(BF16)
    arrived(1, ghost_mine)
    up_send[...] = (own[ghost_mine, :] + theirs[ghost_mine, :]).astype(BF16)
    sides = []
    for i, (src, dst, place) in enumerate(
        ((up_send, from_below, above), (down_send, from_above, below))
    ):
        side = pltpu.make_async_remote_copy(
            src_ref=src, dst_ref=dst.at[here, :],
            send_sem=side_send.at[i], recv_sem=side_recv.at[i],
            device_id=(place, state), device_id_type=MESH,
        )
        side.start()
        sides.append(side)

    for load in loads[1:]:
        load.wait()
    gain, damp, center = coef[0:1, :], coef[8:9, :], coef[16:17, :]

    def step(h, now, before):
        return (h - center * now) * gain - damp * before

    stores = []

    def keep(src, dst, span):
        copy = pltpu.make_async_copy(
            src.at[span, :], dst.at[span, :], store_sem.at[len(stores)]
        )
        copy.start()
        stores.append(copy)

    for i in range(pieces):
        span = spans[i + 2]
        swaps[i + 2].wait_recv()
        new[span, :] = step(own[span, :] + theirs[span, :], cur[span, :], prev[span, :])
        keep(new, out, span)
    arrived(6, face_other)
    arrived(7, ghost_other)
    relays = []
    for i, dst in enumerate((from_below, from_above)):
        sides[i].wait_recv()
        relay = pltpu.make_async_remote_copy(
            src_ref=dst.at[here, :], dst_ref=dst.at[here, :],
            send_sem=relay_send.at[i], recv_sem=relay_recv.at[i],
            device_id=(space, other), device_id_type=MESH,
        )
        relay.start()
        relays.append(relay)

    def finish(face_span, ghost_span, span):
        h = own[face_span, :] + theirs[face_span, :]
        extra = from_below[span, :].astype(F32)
        h = h + jnp.where(space == 0, jnp.zeros_like(extra), extra)
        new[face_span, :] = step(h, cur[face_span, :], prev[face_span, :])
        keep(new, out, face_span)
        h = own[ghost_span, :] + theirs[ghost_span, :] + from_above[span, :].astype(F32)
        h = jnp.where(space == parts - 1, jnp.zeros_like(h), h)
        new_ghost[span, :] = step(h, cur_ghost[span, :], prev_ghost[span, :])
        keep(new_ghost, out_ghost, span)

    finish(face_mine, ghost_mine, here)
    for i, dst in enumerate((from_below, from_above)):
        pltpu.make_async_remote_copy(
            src_ref=dst.at[there, :], dst_ref=dst.at[there, :],
            send_sem=relay_send.at[i], recv_sem=relay_recv.at[i],
            device_id=(space, other), device_id_type=MESH,
        ).wait_recv()
    finish(face_other, ghost_other, there)
    for copy in swaps + sides + relays:
        copy.wait_send()
    for copy in stores:
        copy.wait()


def exchange(coef, part, cur, cur_ghost, prev, prev_ghost, qmain):
    qface = cur_ghost.shape[0]
    parts = lax.axis_size("space")
    hbm = pl.BlockSpec(memory_space=pltpu.HBM)
    half = qface // 2
    return pl.pallas_call(
        functools.partial(exchange_kernel, qmain, qface, parts),
        name="exchange_update",
        out_shape=[
            jax.ShapeDtypeStruct(cur.shape, F32),
            jax.ShapeDtypeStruct(cur_ghost.shape, F32),
        ],
        in_specs=[pl.BlockSpec(memory_space=pltpu.VMEM)] + [hbm] * 5,
        out_specs=[hbm, hbm],
        scratch_shapes=[
            pltpu.VMEM(part.shape, F32),
            pltpu.VMEM(cur.shape, F32),
            pltpu.VMEM(cur_ghost.shape, F32),
            pltpu.VMEM(cur.shape, F32),
            pltpu.VMEM(cur_ghost.shape, F32),
            pltpu.VMEM(part.shape, F32),
            pltpu.VMEM(cur.shape, F32),
            pltpu.VMEM(cur_ghost.shape, F32),
            pltpu.VMEM((half, LANES), BF16),
            pltpu.VMEM((half, LANES), BF16),
            pltpu.VMEM((qface, LANES), BF16),
            pltpu.VMEM((qface, LANES), BF16),
            pltpu.SemaphoreType.DMA((5,)),
            pltpu.SemaphoreType.DMA((8,)),
            pltpu.SemaphoreType.DMA((8,)),
            pltpu.SemaphoreType.DMA((8,)),
            pltpu.SemaphoreType.DMA((2,)),
            pltpu.SemaphoreType.DMA((2,)),
            pltpu.SemaphoreType.DMA((2,)),
            pltpu.SemaphoreType.DMA((2,)),
        ],
        compiler_params=pltpu.CompilerParams(
            collective_id=0, has_side_effects=True, vmem_limit_bytes=VMEM_LIMIT
        ),
    )(coef, part, cur, cur_ghost, prev, prev_ghost)


def margin_kernel(grid, rounded, out, blocks, gram, sums, across, along, *sems):
    depth, width, ring = grid
    space, state = lax.axis_index("space"), lax.axis_index("state")
    z, x = space // width, lax.rem(space, width)
    y, core = state // 2, lax.rem(state, 2)
    chips = ring // 2
    state_send, state_recv, row_send, row_recv, x_send, x_recv, z_send, z_recv = sems
    friends = [(space, lax.rem(state + k, ring)) for k in range(1, ring)]
    x_friends = [(z * width + lax.rem(x + k, width), state) for k in range(1, width)]
    z_friends = [(lax.rem(z + k, depth) * width + x, state) for k in range(1, depth)]
    barrier = pltpu.get_barrier_semaphore()
    everyone = friends + x_friends + z_friends
    for device in everyone:
        pl.semaphore_signal(barrier, inc=1, device_id=device, device_id_type=MESH)
    pl.semaphore_wait(barrier, len(everyone))

    copies = []
    for k in range(1, chips):
        to = lax.rem(y + k, chips)
        copy = pltpu.make_async_remote_copy(
            src_ref=rounded.at[to], dst_ref=blocks.at[k],
            send_sem=state_send.at[k], recv_sem=state_recv.at[k],
            device_id=(space, 2 * to + core), device_id_type=MESH,
        )
        copy.start()
        copies.append(copy)
    blocks[0] = rounded[y]
    for copy in copies:
        copy.wait()
    ordered = jnp.concatenate([blocks[lax.rem(y + chips - i, chips)] for i in range(chips)], axis=0)
    gram[:, : ordered.shape[0]] = lax.dot_general(
        ordered, ordered, (((1,), (1,)), ((), ())), preferred_element_type=F32
    )
    gram[:, ordered.shape[0] :] = jnp.zeros_like(gram[:, ordered.shape[0] :])

    def add_up(sources, friends, slots, send, recv):
        copies = []
        for k, (src, device) in enumerate(zip(sources, friends), 1):
            copy = pltpu.make_async_remote_copy(
                src_ref=src, dst_ref=slots.at[k], send_sem=send.at[k], recv_sem=recv.at[k],
                device_id=device, device_id_type=MESH,
            )
            copy.start()
            copies.append(copy)
        for copy in copies:
            copy.wait()
        return functools.reduce(lambda a, b: a + b, [slots[k] for k in range(1, len(friends) + 1)])

    def rows_of(member):
        return pl.ds(pl.multiple_of(member * 8, 8), 8)

    rows = [gram.at[rows_of(device[1]), :] for device in friends]
    total = gram[rows_of(state), :] + add_up(rows, friends, sums, row_send, row_recv)
    across[0] = total
    total = total + add_up([across.at[0]] * (width - 1), x_friends, across, x_send, x_recv)
    along[0] = total
    total = total + add_up([along.at[0]] * (depth - 1), z_friends, along, z_send, z_recv)
    out[...] = total[:, : out.shape[1]]


def margin_of(rounded):
    ring = lax.axis_size("state")
    parts = lax.axis_size("space")
    width = 4
    depth = parts // width
    chips = ring // 2
    count = 8 * ring
    vmem = pl.BlockSpec(memory_space=pltpu.VMEM)
    sems = [pltpu.SemaphoreType.DMA((n,)) for n in (chips, chips, ring, ring, width, width, depth, depth)]
    return pl.pallas_call(
        functools.partial(margin_kernel, (depth, width, ring)),
        name="margin_rows",
        out_shape=jax.ShapeDtypeStruct((8, count), F32),
        in_specs=[vmem],
        out_specs=vmem,
        scratch_shapes=[
            pltpu.VMEM(rounded.shape, BF16),
            pltpu.VMEM((count, LANES), F32),
            pltpu.VMEM((ring, 8, LANES), F32),
            pltpu.VMEM((width, 8, LANES), F32),
            pltpu.VMEM((depth, 8, LANES), F32),
        ]
        + sems,
        compiler_params=pltpu.CompilerParams(
            collective_id=1, has_side_effects=True, vmem_limit_bytes=VMEM_LIMIT
        ),
    )(rounded)


def final_kernel(qmain, qface, core_ref, mainface, face_hbm, emat, out, rounded, X, R, sems, *faces):
    copies = start_faces(face_hbm, faces, sems)
    expand_section(mainface, 0, X, 0, qmain, emat)
    expand_section(mainface, qmain, R, 0, qface, emat)
    for copy in copies:
        copy.wait()

    def put(q, carry):
        for j, n in enumerate(faces_at(faces, qface, q)):
            X[pl.ds(n, 1), :] = R[pl.ds(j * qface + q, 1), :]
        return carry

    lax.fori_loop(0, qface, put, 0, unroll=4)
    core = core_ref[0]

    def turn(i, carry):
        q = pl.multiple_of(i * 128, 128)
        rows = merge_groups([X[pl.ds(j * qmain + q, 128), :] for j in range(G)]).T
        for j in range(G):
            a = rows[j * W : j * W + 8]
            b = rows[j * W + 8 : j * W + 16]
            out[:, pl.ds(j * qmain + q, 128)] = jnp.where(core == 0, a, b)
        far = G // 2
        for j in range(far):
            a = rows[j * W : (j + 1) * W]
            b = rows[(far + j) * W : (far + j + 1) * W]
            rounded[j, :, pl.ds(q, 128)] = jnp.where(core == 0, a, b).astype(BF16)
        return carry

    lax.fori_loop(0, qmain // 128, turn, 0)


def final(core, mainface, face_nodes, emat, qmain):
    qface = mainface.shape[0] - qmain
    vmem = pl.BlockSpec(memory_space=pltpu.VMEM)
    return pl.pallas_call(
        functools.partial(final_kernel, qmain, qface),
        name="final_block",
        out_shape=[
            jax.ShapeDtypeStruct((8, G * qmain), F32),
            jax.ShapeDtypeStruct((G // 2, W, qmain), BF16),
        ],
        in_specs=[
            pl.BlockSpec(memory_space=pltpu.SMEM), vmem, pl.BlockSpec(memory_space=pl.ANY), vmem
        ],
        out_specs=[vmem, vmem],
        scratch_shapes=[
            pltpu.VMEM((G * qmain, LANES), F32),
            pltpu.VMEM((G * qface, LANES), F32),
            pltpu.SemaphoreType.DMA((G * qface // FACE_LIST,)),
        ]
        + [pltpu.SMEM((FACE_LIST,), jnp.int32)] * (G * qface // FACE_LIST),
        compiler_params=pltpu.CompilerParams(vmem_limit_bytes=VMEM_LIMIT),
    )(core, mainface, face_nodes, emat)


def body(states, bounds, element_matrix, elem_nodes, face_nodes, kinetic, potential, elem_count):
    parts = lax.axis_size("space")
    members = lax.axis_size("state")
    core = lax.rem(lax.axis_index("state"), 2)
    npe, slot_count = elem_nodes.shape
    half = slot_count // 2
    chunks = half // G
    steps = npe // KU
    qmain = states.shape[1] // G

    mine = lax.dynamic_slice(elem_nodes, (0, core * half), (npe, half))
    raw = mine.reshape(KU, steps, G, chunks).transpose(0, 2, 3, 1).reshape(KU * G, chunks * steps)
    emat, fmat = expand_matrix(), fold_matrix()
    which = core.reshape(1)

    partner = lax.ppermute(states, "state", [(i, i ^ 1) for i in range(members)])
    cur, face_high, face_low = states_rows(which, states, partner, face_nodes, emat)
    downwards = [(i, i - 1) for i in range(1, parts)]
    ghost_high = lax.ppermute(face_high, "space", downwards)
    ghost_low = lax.ppermute(face_low, "space", downwards)
    slots, scales, mcat, *coefs = prepare(
        face_low, which, elem_count, bounds, raw, face_nodes, element_matrix, kinetic, potential,
        states.shape[1], chunks,
    )
    ghost_high, ghost_low = ghost_high.astype(F32), ghost_low.astype(F32)
    prev, prev_ghost = cur, ghost_high + ghost_low
    for k in range(DEG):
        ghost = new_ghost if k else ghost_high
        part = elements(cur, ghost, slots, mcat, scales, emat, fmat, qmain, steps)
        cur_ghost = ghost if k else prev_ghost
        new, new_ghost = exchange(coefs[k], part, cur, cur_ghost, prev, prev_ghost, qmain)
        prev, prev_ghost, cur = cur, cur_ghost, new
    filtered, rounded = final(which, cur, face_nodes, emat, qmain)
    margin = margin_of(rounded) / (states.shape[1] * parts)
    return filtered, margin


def solution(mesh):
    in_specs = (
        P("state", "space"),
        P(),
        P(),
        P(None, "space"),
        P("space"),
        P("space"),
        P("space"),
        P("space"),
    )
    out_specs = (P("state", "space"), P("state", None))
    return jax.shard_map(body, mesh=mesh, in_specs=in_specs, out_specs=out_specs, check_vma=False)
```
